512 devices in a mesh: dp: 64 (over y, z_lo, x), inner: 8 (over z_hi, core).
Axes of the slice: x: 4, y: 8, z: 8 (z_hi: 4, z_lo: 2; z = z_hi * 2 + z_lo), core: 2. Of those that a mesh axis runs over, the one named last changes fastest.
Arguments:
- images: float32 [131072, 1152], P(('dp', 'inner')), may hold values from -6 to 6
- texts: float32 [131072, 1152], P(('dp', 'inner')), may hold values from -6 to 6
- image_cluster: int32 [131072], P(('dp', 'inner')), may hold values from 0 to 15
- text_cluster: int32 [131072], P(('dp', 'inner')), may hold values from 0 to 15
- text_pair: int32 [131072], P(('dp', 'inner')), may hold values from 0 to 131071, as said below
- logit_scale: float32 [], replicated, may hold values from 0.05 to 0.1
- logit_bias: float32 [], replicated, may hold values from -3 to -1
Outputs:
- image_grad: float32 [131072, 1152], P(('dp', 'inner'))
- text_grad: float32 [131072, 1152], P(('dp', 'inner'))
The draws below stay inside these ranges and needn't reach their ends.
Inputs may be any that keep to these rules, and one draw needn't show every extreme that they name: `text_pair`: for a text in block (a, k), its true image lies in one of the blocks (a, k), ((a - 1) mod 64, k), (a, (k + 1) mod 8), ((a - 1) mod 64, (k + 1) mod 8).
All inputs are finite; a program needn't handle non-finite values.
Results may differ from the reference program's by a relative error of at most 0.0003.
Values sent between devices are 32-bit elements; how exact they have to be, the bound alone decides.
A program may use at most 64 MiB of HBM per device.

```python
import math
import jax
import jax.numpy as jnp
from jax import lax

D = 1152
ROWS = 256
CLUSTERS = 16
OUTER_BLOCKS = 64
INNER_BLOCKS = 8
IMAGES = 131072


def draw_text_pair(key, part):
    key = jax.random.fold_in(key, 7)
    first_key, second_key, third_key = jax.random.split(key, 3)
    positions = jnp.arange(IMAGES, dtype=jnp.int32)
    block_number = positions // ROWS
    outer_coord = block_number // INNER_BLOCKS
    inner_coord = block_number % INNER_BLOCKS
    ends = (positions == 0) | (positions == IMAGES - 1)
    outer_offset = jax.random.randint(first_key, (IMAGES,), 0, 2, dtype=jnp.int32)
    inner_offset = jax.random.randint(second_key, (IMAGES,), 0, 2, dtype=jnp.int32)
    row_within = jax.random.randint(third_key, (IMAGES,), 0, ROWS, dtype=jnp.int32)
    outer_offset = jnp.where(ends, 0, outer_offset)
    inner_offset = jnp.where(ends, 0, inner_offset)
    row_within = jnp.where(positions == 0, 0, jnp.where(positions == IMAGES - 1, ROWS - 1, row_within))
    image_block = (outer_coord - outer_offset) % OUTER_BLOCKS * INNER_BLOCKS + (inner_coord + inner_offset) % INNER_BLOCKS
    return (image_block * ROWS + row_within).astype(jnp.int32)


def with_ends(entries, own_key, low, largest):
    shape = entries.shape
    index_at = [jax.random.randint(jax.random.fold_in(own_key, axis), (), 0, shape[axis]) for axis in range(len(shape))]
    entries = entries.at[tuple(index_at)].set(low)
    longest = shape.index(max(shape))
    index_at[longest] = (index_at[longest] + 1) % shape[longest]
    return entries.at[tuple(index_at)].set(largest)


def levels(key, extent, cuts, least, top_value):
    gain = 1.0
    for axis_at, blocks in cuts:
        heights = jax.random.uniform(jax.random.fold_in(jax.random.fold_in(key, 6), axis_at), (blocks,), jnp.float32, least / len(cuts), top_value / len(cuts))
        gain = gain * jnp.repeat(jnp.exp(heights), extent[axis_at] // blocks).reshape((-1,) + (1,) * (len(extent) - 1 - axis_at))
    return gain


def scatter_about(key, shape, spread, most, cuts=(), held_as=jnp.bfloat16):
    entries = spread * jax.random.normal(key, shape, jnp.float32)
    if cuts:
        entries = entries * levels(key, shape, cuts, -0.22, 0.18)
    return jnp.clip(entries, -most, most).astype(held_as)


def setup_inputs(seed: int = 0) -> dict:
    key_of = jax.random.split(jax.random.key(seed), 8)
    images = scatter_about(key_of[0], (IMAGES, D), 1.0, 6.0, ((0, 512),), jnp.float32)
    texts = scatter_about(key_of[1], (IMAGES, D), 1.0, 6.0, ((0, 512),), jnp.float32)
    image_cluster = with_ends(jax.random.randint(key_of[2], (IMAGES,), 0, CLUSTERS), jax.random.fold_in(key_of[2], 1), 0, CLUSTERS - 1).astype(jnp.int32)
    text_cluster = with_ends(jax.random.randint(key_of[3], (IMAGES,), 0, CLUSTERS), jax.random.fold_in(key_of[3], 1), 0, CLUSTERS - 1).astype(jnp.int32)
    text_pair = draw_text_pair(jax.random.fold_in(key_of[7], 71), 0)
    logit_scale = jnp.clip(jnp.exp(jax.random.uniform(key_of[5], (), jnp.float32, math.log(0.05), math.log(0.1))), 0.05, 0.1)
    logit_bias = jnp.clip(jax.random.uniform(key_of[6], (), jnp.float32, -3.0, -1.0), -3.0, -1.0)
    return {"images": images, "texts": texts, "image_cluster": image_cluster, "text_cluster": text_cluster, "text_pair": text_pair, "logit_scale": logit_scale, "logit_bias": logit_bias}


highest_precision = lax.Precision.HIGHEST


def pair_grads(pieces, scale_value, bias_value):
    image_rows, text_rows, image_ids, text_ids, text_owner, first_image = pieces
    logits = scale_value * jnp.dot(image_rows, text_rows.T, precision=highest_precision, preferred_element_type=jnp.float32) + bias_value
    numbers = first_image + jnp.arange(image_rows.shape[0], dtype=jnp.int32)
    positive = text_owner[None, :] == numbers[:, None]
    keep_pair = positive | (image_ids[:, None] != text_ids[None, :])
    labels = jnp.where(positive, 1.0, -1.0)
    weights = jnp.where(keep_pair, -labels * jax.nn.sigmoid(-labels * logits), 0.0)
    image_part = scale_value * jnp.dot(weights, text_rows, precision=highest_precision, preferred_element_type=jnp.float32)
    text_part = scale_value * jnp.dot(weights.T, image_rows, precision=highest_precision, preferred_element_type=jnp.float32)
    return image_part, text_part


def reference(images, texts, image_cluster, text_cluster, text_pair, logit_scale, logit_bias):
    block_count = OUTER_BLOCKS * INNER_BLOCKS

    def blocks(array):
        return array.reshape((OUTER_BLOCKS, INNER_BLOCKS) + array.shape[1:])

    def flatten_blocks(array):
        return array.reshape((block_count,) + array.shape[2:])

    image_blocks = blocks(images.reshape(block_count, ROWS, D))
    image_ids = blocks(image_cluster.reshape(block_count, ROWS))
    text_blocks = blocks(texts.reshape(block_count, ROWS, D))
    text_ids = blocks(text_cluster.reshape(block_count, ROWS))
    text_owner = blocks(text_pair.reshape(block_count, ROWS))
    firsts = jnp.arange(block_count, dtype=jnp.int32) * ROWS
    image_total = jnp.zeros((OUTER_BLOCKS, INNER_BLOCKS, ROWS, D), jnp.float32)
    text_total = jnp.zeros((OUTER_BLOCKS, INNER_BLOCKS, ROWS, D), jnp.float32)
    for outer_step in range(2):
        for visit_step in range(2):
            shifts = (-outer_step, visit_step)
            moved_texts = jnp.roll(text_blocks, shifts, axis=(0, 1))
            moved_ids = jnp.roll(text_ids, shifts, axis=(0, 1))
            moved_owner = jnp.roll(text_owner, shifts, axis=(0, 1))
            pieces = (flatten_blocks(image_blocks), flatten_blocks(moved_texts), flatten_blocks(image_ids),
                      flatten_blocks(moved_ids), flatten_blocks(moved_owner), firsts)
            image_part, text_part = lax.map(lambda piece: pair_grads(piece, logit_scale, logit_bias), pieces)
            image_total = image_total + blocks(image_part)
            text_total = text_total + jnp.roll(blocks(text_part), (outer_step, -visit_step), axis=(0, 1))
    return image_total.reshape(IMAGES, D), text_total.reshape(IMAGES, D)
```

```python
import functools

import jax
import jax.numpy as jnp
from jax import lax
from jax.experimental import pallas as pl
from jax.experimental.pallas import tpu as pltpu
from jax.sharding import PartitionSpec as P

MESH = pl.DeviceIdType.MESH
CHUNKS = 4
RUN = 4


def split(value):
    high = value.astype(jnp.bfloat16)
    low = (value - high.astype(jnp.float32)).astype(jnp.bfloat16)
    return high, low


def dot(left, right, dims):
    return lax.dot_general(left, right, (dims, ((), ())), preferred_element_type=jnp.float32)


def dot3(left, right, dims):
    return (
        dot(left[0], right[0], dims)
        + dot(left[0], right[1], dims)
        + dot(left[1], right[0], dims)
    )


NT = ((1,), (1,))
NN = ((1,), (0,))


def kernel(
    dp_count, inner_count,
    img, txt, img_cluster, txt_cluster, txt_pair, scale_ref, bias_ref,
    grad_out, back_out,
    home, visit, high, low, grad, visit_grad, weight, meta, visit_meta, column,
    relay_out, relay_back,
    load_sem, store_sem, fwd_send, fwd_recv, meta_send, meta_recv,
    back_send, back_recv, relay_send, relay_recv, go_sem,
):
    rows, width = img.shape
    step = rows // CHUNKS
    a, k = lax.axis_index("dp"), lax.axis_index("inner")
    x = a % RUN
    run = a - x
    core = k % 2
    dp_next, dp_prev = (a + 1) % dp_count, (a + dp_count - 1) % dp_count
    in_next, in_prev = (k + 1) % inner_count, (k + inner_count - 1) % inner_count
    run_next, run_prev = (run + RUN) % dp_count, (run + dp_count - 1) % dp_count
    early, late = core, 1 - core
    scale, bias = scale_ref[0], bias_ref[0]

    loads = [
        pltpu.make_async_copy(img, home.at[0], load_sem.at[0]),
        pltpu.make_async_copy(txt, home.at[1], load_sem.at[1]),
    ]
    for load in loads:
        load.start()

    barrier = pltpu.get_barrier_semaphore()

    def greet(dp, inner):
        pl.semaphore_signal(barrier, inc=1, device_id=(dp, inner), device_id_type=MESH)

    for other in range(1, RUN):
        greet(run + (x + other) % RUN, k)
    greet(a, in_next)
    greet(a, in_prev)
    greet(run_next, k)
    greet(run_prev, k)

    @pl.when(x == 0)
    def _():
        for other in range(2, RUN + 1):
            greet((run + dp_count - other) % dp_count, k)

    @pl.when(x == RUN - 1)
    def _():
        for other in range(1, RUN):
            greet((run + RUN + other) % dp_count, k)

    row = lax.broadcasted_iota(jnp.int32, (8, rows), 0)
    number = (a * inner_count + k) * rows + lax.broadcasted_iota(jnp.int32, (8, rows), 1)
    wide = lambda ref: jnp.broadcast_to(ref[...], (8, rows))
    meta[0] = jnp.where(row == 0, number, wide(img_cluster)).astype(jnp.float32)
    meta[1] = jnp.where(row == 0, wide(txt_pair), wide(txt_cluster)).astype(jnp.float32)

    end = (x == 0) | (x == RUN - 1)
    pl.semaphore_wait(barrier, jnp.where(end, 2 * RUN + 2, RUN + 3))

    def piece(chunk):
        return pl.ds(pl.multiple_of(chunk * step, step), step)

    def remote(src, dst, send, recv, dp, inner):
        return pltpu.make_async_remote_copy(
            src_ref=src, dst_ref=dst, send_sem=send, recv_sem=recv,
            device_id=(dp, inner), device_id_type=MESH,
        )

    meta_copies = [
        remote(meta.at[0], visit_meta.at[0], meta_send.at[0], meta_recv.at[0], dp_next, k),
        remote(meta.at[1], visit_meta.at[1], meta_send.at[1], meta_recv.at[1], a, in_next),
    ]

    def image_direct(chunk):
        return remote(
            img.at[piece(chunk)], visit.at[0, piece(chunk)],
            fwd_send.at[0, chunk], fwd_recv.at[0, chunk], dp_next, k,
        )

    def image_start(chunk):
        if chunk == 0:
            image_direct(chunk).start()
            return

        @pl.when(x < RUN - 1)
        def _():
            image_direct(chunk).start()

        @pl.when(x == RUN - 1)
        def _():
            remote(
                img.at[piece(chunk)], relay_out,
                fwd_send.at[0, chunk], relay_recv.at[0], run + chunk - 1, k,
            ).start()

    def text_copy(chunk):
        return remote(
            txt.at[piece(chunk)], visit.at[1, piece(chunk)],
            fwd_send.at[1, chunk], fwd_recv.at[1, chunk], a, in_next,
        )

    def relay_out_copy():
        chunk = (x + 1) % CHUNKS
        return remote(
            relay_out, visit.at[0, piece(chunk)],
            relay_send.at[0], fwd_recv.at[0, chunk], run_next, k,
        )

    def relay_out_step():
        @pl.when(x < RUN - 1)
        def _():
            remote(relay_out, relay_out, relay_send.at[0], relay_recv.at[0], run_next, k).wait_recv()
            relay_out_copy().start()

    def image_back_direct(chunk):
        return remote(
            visit_grad.at[0, piece(chunk)], back_out.at[0, piece(chunk)],
            back_send.at[0, chunk], back_recv.at[0, chunk], dp_prev, k,
        )

    def image_back_start(chunk):
        aside = (x == 0) & (chunk > 0)

        @pl.when(jnp.logical_not(aside))
        def _():
            image_back_direct(chunk).start()

        @pl.when(aside)
        def _():
            remote(
                visit_grad.at[0, piece(chunk)], relay_back,
                back_send.at[0, chunk], relay_recv.at[1], run + chunk, k,
            ).start()

    def relay_back_copy():
        return remote(
            relay_back, back_out.at[0, piece(x)],
            relay_send.at[1], back_recv.at[0, x], run_prev, k,
        )

    def relay_back_step():
        @pl.when(x > 0)
        def _():
            remote(relay_back, relay_back, relay_send.at[1], relay_recv.at[1], run_prev, k).wait_recv()
            relay_back_copy().start()

    def text_back(chunk):
        return remote(
            visit_grad.at[1, piece(chunk)], back_out.at[1, piece(chunk)],
            back_send.at[1, chunk], back_recv.at[1, chunk], a, in_prev,
        )

    def fwd_wait(which, chunk):
        pltpu.make_async_copy(
            visit.at[which, piece(chunk)], visit.at[which, piece(chunk)], fwd_recv.at[which, chunk]
        ).wait()

    def weights(logits, left, right):
        logits = scale * logits + bias
        positive = left[:, 0:1] == right[0:1, :]
        other = left[:, 1:2] != right[1:2, :]
        sig = jax.nn.sigmoid(jnp.where(positive, -logits, logits))
        return scale * jnp.where(positive, -sig, jnp.where(other, sig, 0.0))

    for copy in meta_copies:
        copy.start()

    @pl.when(core == 0)
    def _():
        for chunk in range(CHUNKS):
            image_start(chunk)

    for chunk in range(CHUNKS):
        text_copy(chunk).start()

    near, far = pl.ds(0, rows), pl.ds(rows, rows)
    for which in range(2):
        loads[which].wait()
        high[which, near], low[which, near] = split(home[which])
    early_near = (high[early, near], low[early, near])
    late_near = (high[late, near], low[late, near])
    column[0] = jnp.transpose(meta[late])
    pair = weights(dot3(late_near, early_near, NT), column[0], meta[early])
    grad[late] = dot3(split(pair), early_near, NN)
    grad[early] = dot3(split(pair.T), late_near, NN)

    @pl.when(core == 0)
    def _():
        relay_out_step()
        for chunk in range(CHUNKS):
            image_direct(chunk).wait_send()
        pl.semaphore_signal(go_sem, inc=1, device_id=(a, in_next), device_id_type=MESH)

    pltpu.make_async_copy(visit_meta.at[early], visit_meta.at[early], meta_recv.at[early]).wait()
    for chunk in range(CHUNKS):
        fwd_wait(early, chunk)
    high[early, far], low[early, far] = split(visit[early])
    early_far = (high[early, far], low[early, far])
    late_near = (high[late, near], low[late, near])
    pair = weights(dot3(late_near, early_far, NT), column[0], visit_meta[early])
    grad[late] += dot3(split(pair), early_far, NN)
    visit_grad[early] = dot3(split(pair.T), late_near, NN)

    @pl.when(core == 1)
    def _():
        pl.semaphore_wait(go_sem, 1)
        for chunk in range(CHUNKS):
            image_start(chunk)
        relay_out_step()

    pltpu.make_async_copy(visit_meta.at[late], visit_meta.at[late], meta_recv.at[late]).wait()
    column[1] = jnp.transpose(visit_meta[late])

    def late_chunk(chunk, carry):
        fwd_wait(late, chunk)
        here = piece(chunk)
        there = pl.ds(pl.multiple_of(rows + chunk * step, step), step)
        part = split(visit[late, here])
        high[late, there], low[late, there] = part
        both = (high[early], low[early])
        right = jnp.concatenate([meta[early], visit_meta[early]], axis=1)
        pair = weights(dot3(part, both, NT), column[1, here], right)
        weight[here] = pair
        visit_grad[late, here] = dot3(split(pair), both, NN)

        @pl.when(core == 0)
        def _():
            text_back(chunk).start()

        @pl.when(core == 1)
        def _():
            image_back_start(chunk)

        return carry

    lax.fori_loop(0, CHUNKS, late_chunk, 0)

    @pl.when(core == 1)
    def _():
        relay_back_step()

    late_far = (high[late, far], low[late, far])

    visit_grad[early] += dot3(split(weight[:, rows:].T), late_far, NN)

    @pl.when(core == 0)
    def _():
        for chunk in range(CHUNKS):
            image_back_start(chunk)

    @pl.when(core == 1)
    def _():
        for chunk in range(CHUNKS):
            text_back(chunk).start()

    grad[early] += dot3(split(weight[:, :rows].T), late_far, NN)
    store = pltpu.make_async_copy(grad, grad_out, store_sem)
    store.start()

    @pl.when(core == 0)
    def _():
        relay_back_step()

    for which in range(2):
        for chunk in range(CHUNKS):
            pltpu.make_async_copy(
                back_out.at[which, piece(chunk)], back_out.at[which, piece(chunk)],
                back_recv.at[which, chunk],
            ).wait()

    @pl.when(core == 1)
    def _():
        for chunk in range(CHUNKS):
            image_direct(chunk).wait_send()

    for chunk in range(CHUNKS):
        text_copy(chunk).wait_send()
        text_back(chunk).wait_send()
        image_back_direct(chunk).wait_send()
    for copy in meta_copies:
        copy.wait_send()

    @pl.when(x < RUN - 1)
    def _():
        relay_out_copy().wait_send()

    @pl.when(x > 0)
    def _():
        relay_back_copy().wait_send()

    store.wait()


def body(images, texts, image_cluster, text_cluster, text_pair, logit_scale, logit_bias):
    rows, width = images.shape
    step = rows // CHUNKS
    dp_count, inner_count = lax.axis_size("dp"), lax.axis_size("inner")
    dma = pltpu.SemaphoreType.DMA
    f32, bf16 = jnp.float32, jnp.bfloat16
    hbm, vmem, smem = (
        pl.BlockSpec(memory_space=space) for space in (pl.ANY, pltpu.VMEM, pltpu.SMEM)
    )
    grads = jax.ShapeDtypeStruct((2, rows, width), f32)
    own, back = pl.pallas_call(
        functools.partial(kernel, dp_count, inner_count),
        out_shape=(grads, grads),
        in_specs=[hbm, hbm, vmem, vmem, vmem, smem, smem],
        out_specs=(hbm, hbm),
        scratch_shapes=[
            pltpu.VMEM((2, rows, width), f32),
            pltpu.VMEM((2, rows, width), f32),
            pltpu.VMEM((2, 2 * rows, width), bf16),
            pltpu.VMEM((2, 2 * rows, width), bf16),
            pltpu.VMEM((2, rows, width), f32),
            pltpu.VMEM((2, rows, width), f32),
            pltpu.VMEM((rows, 2 * rows), f32),
            pltpu.VMEM((2, 8, rows), f32),
            pltpu.VMEM((2, 8, rows), f32),
            pltpu.VMEM((2, rows, 8), f32),
            pltpu.VMEM((step, width), f32),
            pltpu.VMEM((step, width), f32),
            dma((2,)),
            dma,
            dma((2, CHUNKS)),
            dma((2, CHUNKS)),
            dma((2,)),
            dma((2,)),
            dma((2, CHUNKS)),
            dma((2, CHUNKS)),
            dma((2,)),
            dma((2,)),
            pltpu.SemaphoreType.REGULAR,
        ],
        compiler_params=pltpu.CompilerParams(
            collective_id=0, has_side_effects=True, vmem_limit_bytes=48 * 1024 * 1024
        ),
        cost_estimate=pl.CostEstimate(
            flops=24 * rows * rows * width, bytes_accessed=24 * rows * width, transcendentals=0
        ),
    )(
        images, texts,
        image_cluster.reshape(1, rows), text_cluster.reshape(1, rows), text_pair.reshape(1, rows),
        logit_scale.reshape(1), logit_bias.reshape(1),
    )
    return (own[0] + back[0], own[1] + back[1])


def solution(mesh):
    return jax.shard_map(
        body,
        mesh=mesh,
        in_specs=(
            P(("dp", "inner"), None),
            P(("dp", "inner"), None),
            P(("dp", "inner")),
            P(("dp", "inner")),
            P(("dp", "inner")),
            P(),
            P(),
        ),
        out_specs=(P(("dp", "inner"), None), P(("dp", "inner"), None)),
        check_vma=False,
    )
```

```python
import functools

import jax
import jax.numpy as jnp
from jax import lax
from jax.experimental import pallas as pl
from jax.experimental.pallas import tpu as pltpu
from jax.sharding import PartitionSpec as P

MESH = pl.DeviceIdType.MESH
CHUNKS = 4
RUN = 4


def split(value):
    high = value.astype(jnp.bfloat16)
    low = (value - high.astype(jnp.float32)).astype(jnp.bfloat16)
    return high, low


def dot(left, right, dims):
    return lax.dot_general(left, right, (dims, ((), ())), preferred_element_type=jnp.float32)


def dot3(left, right, dims):
    return (
        dot(left[0], right[0], dims)
        + dot(left[0], right[1], dims)
        + dot(left[1], right[0], dims)
    )


NT = ((1,), (1,))
NN = ((1,), (0,))


def kernel(
    dp_count, inner_count,
    img, txt, img_cluster_in, txt_cluster_in, txt_pair_in, scale_ref, bias_ref,
    grad_out, back_out,
    home, ids, visit, high, low, grad, visit_grad, meta, visit_meta, column,
    relay_out, relay_back,
    load_sem, store_sem, fwd_send, fwd_recv, meta_send, meta_recv,
    back_send, back_recv, relay_send, relay_recv, go_sem,
):
    rows, width = img.shape
    step = rows // CHUNKS
    a, k = lax.axis_index("dp"), lax.axis_index("inner")
    x = a % RUN
    run = a - x
    core = k % 2
    dp_next, dp_prev = (a + 1) % dp_count, (a + dp_count - 1) % dp_count
    in_next, in_prev = (k + 1) % inner_count, (k + inner_count - 1) % inner_count
    run_next, run_prev = (run + RUN) % dp_count, (run + dp_count - 1) % dp_count
    early, late = core, 1 - core
    scale, bias = scale_ref[0], bias_ref[0]

    loads = [
        pltpu.make_async_copy(img, home.at[0], load_sem.at[0]),
        pltpu.make_async_copy(txt, home.at[1], load_sem.at[1]),
        pltpu.make_async_copy(img_cluster_in, ids.at[0], load_sem.at[2]),
        pltpu.make_async_copy(txt_cluster_in, ids.at[1], load_sem.at[3]),
        pltpu.make_async_copy(txt_pair_in, ids.at[2], load_sem.at[4]),
    ]
    for load in loads:
        load.start()

    barrier = pltpu.get_barrier_semaphore()

    def greet(dp, inner):
        pl.semaphore_signal(barrier, inc=1, device_id=(dp, inner), device_id_type=MESH)

    for other in range(1, RUN):
        greet(run + (x + other) % RUN, k)
    greet(a, in_next)
    greet(a, in_prev)
    greet(run_next, k)
    greet(run_prev, k)

    @pl.when(x == 0)
    def _():
        for other in range(2, RUN + 1):
            greet((run + dp_count - other) % dp_count, k)

    @pl.when(x == RUN - 1)
    def _():
        for other in range(1, RUN):
            greet((run + RUN + other) % dp_count, k)

    row = lax.broadcasted_iota(jnp.int32, (8, rows), 0)
    number = (a * inner_count + k) * rows + lax.broadcasted_iota(jnp.int32, (8, rows), 1)
    for load in loads[2:]:
        load.wait()
    wide = lambda slot: jnp.broadcast_to(ids[slot], (8, rows))
    meta[0] = jnp.where(row == 0, number, wide(0)).astype(jnp.float32)
    meta[1] = jnp.where(row == 0, wide(2), wide(1)).astype(jnp.float32)

    end = (x == 0) | (x == RUN - 1)
    pl.semaphore_wait(barrier, jnp.where(end, 2 * RUN + 2, RUN + 3))

    def piece(chunk):
        return pl.ds(pl.multiple_of(chunk * step, step), step)

    def remote(src, dst, send, recv, dp, inner):
        return pltpu.make_async_remote_copy(
            src_ref=src, dst_ref=dst, send_sem=send, recv_sem=recv,
            device_id=(dp, inner), device_id_type=MESH,
        )

    meta_copies = [
        remote(meta.at[0], visit_meta.at[0], meta_send.at[0], meta_recv.at[0], dp_next, k),
        remote(meta.at[1], visit_meta.at[1], meta_send.at[1], meta_recv.at[1], a, in_next),
    ]

    def image_direct(chunk):
        return remote(
            img.at[piece(chunk)], visit.at[0, piece(chunk)],
            fwd_send.at[0, chunk], fwd_recv.at[0, chunk], dp_next, k,
        )

    def image_start(chunk):
        if chunk == 0:
            image_direct(chunk).start()
            return

        @pl.when(x < RUN - 1)
        def _():
            image_direct(chunk).start()

        @pl.when(x == RUN - 1)
        def _():
            remote(
                img.at[piece(chunk)], relay_out,
                fwd_send.at[0, chunk], relay_recv.at[0], run + chunk - 1, k,
            ).start()

    def text_copy(chunk):
        return remote(
            txt.at[piece(chunk)], visit.at[1, piece(chunk)],
            fwd_send.at[1, chunk], fwd_recv.at[1, chunk], a, in_next,
        )

    def relay_out_copy():
        chunk = (x + 1) % CHUNKS
        return remote(
            relay_out, visit.at[0, piece(chunk)],
            relay_send.at[0], fwd_recv.at[0, chunk], run_next, k,
        )

    def relay_out_step():
        @pl.when(x < RUN - 1)
        def _():
            remote(relay_out, relay_out, relay_send.at[0], relay_recv.at[0], run_next, k).wait_recv()
            relay_out_copy().start()

    def image_back_direct(chunk):
        return remote(
            visit_grad.at[0, piece(chunk)], back_out.at[0, piece(chunk)],
            back_send.at[0, chunk], back_recv.at[0, chunk], dp_prev, k,
        )

    def image_back_start(chunk):
        aside = (x == 0) & (chunk > 0)

        @pl.when(jnp.logical_not(aside))
        def _():
            image_back_direct(chunk).start()

        @pl.when(aside)
        def _():
            remote(
                visit_grad.at[0, piece(chunk)], relay_back,
                back_send.at[0, chunk], relay_recv.at[1], run + chunk, k,
            ).start()

    def relay_back_copy():
        return remote(
            relay_back, back_out.at[0, piece(x)],
            relay_send.at[1], back_recv.at[0, x], run_prev, k,
        )

    def relay_back_step():
        @pl.when(x > 0)
        def _():
            remote(relay_back, relay_back, relay_send.at[1], relay_recv.at[1], run_prev, k).wait_recv()
            relay_back_copy().start()

    def text_back(chunk):
        return remote(
            visit_grad.at[1, piece(chunk)], back_out.at[1, piece(chunk)],
            back_send.at[1, chunk], back_recv.at[1, chunk], a, in_prev,
        )

    def fwd_wait(which, chunk):
        pltpu.make_async_copy(
            visit.at[which, piece(chunk)], visit.at[which, piece(chunk)], fwd_recv.at[which, chunk]
        ).wait()

    def weights(logits, left, right):
        logits = scale * logits + bias
        positive = left[:, 0:1] == right[0:1, :]
        other = left[:, 1:2] != right[1:2, :]
        sig = jax.nn.sigmoid(jnp.where(positive, -logits, logits))
        return scale * jnp.where(positive, -sig, jnp.where(other, sig, 0.0))

    for copy in meta_copies:
        copy.start()

    @pl.when((core == 0) | (x == RUN - 1))
    def _():
        for chunk in range(CHUNKS):
            image_start(chunk)

    for chunk in range(CHUNKS):
        text_copy(chunk).start()

    near, far = pl.ds(0, rows), pl.ds(rows, rows)
    for which in range(2):
        loads[which].wait()
        high[which, near], low[which, near] = split(home[which])
    early_near = (high[early, near], low[early, near])
    late_near = (high[late, near], low[late, near])
    column[0] = jnp.transpose(meta[late])
    pair = weights(dot3(late_near, early_near, NT), column[0], meta[early])
    grad[late] = dot3(split(pair), early_near, NN)
    grad[early] = dot3(split(pair.T), late_near, NN)

    @pl.when(core == 0)
    def _():
        relay_out_step()
        for chunk in range(CHUNKS):
            image_direct(chunk).wait_send()

        @pl.when(x < RUN - 1)
        def _():
            pl.semaphore_signal(go_sem, inc=1, device_id=(a, in_next), device_id_type=MESH)

    pltpu.make_async_copy(visit_meta.at[early], visit_meta.at[early], meta_recv.at[early]).wait()
    for chunk in range(CHUNKS):
        fwd_wait(early, chunk)
    high[early, far], low[early, far] = split(visit[early])
    early_far = (high[early, far], low[early, far])
    late_near = (high[late, near], low[late, near])
    pair = weights(dot3(late_near, early_far, NT), column[0], visit_meta[early])
    grad[late] += dot3(split(pair), early_far, NN)
    visit_grad[early] = dot3(split(pair.T), late_near, NN)

    @pl.when(core == 1)
    def _():
        relay_out_step()

        @pl.when(x < RUN - 1)
        def _():
            pl.semaphore_wait(go_sem, 1)
            for chunk in range(CHUNKS):
                image_direct(chunk).start()

    pltpu.make_async_copy(visit_meta.at[late], visit_meta.at[late], meta_recv.at[late]).wait()
    column[1] = jnp.transpose(visit_meta[late])

    def late_chunk(chunk, carry):
        fwd_wait(late, chunk)
        here = piece(chunk)
        part = split(visit[late, here])
        both = (high[early], low[early])
        right = jnp.concatenate([meta[early], visit_meta[early]], axis=1)
        pair = weights(dot3(part, both, NT), column[1, here], right)
        visit_grad[late, here] = dot3(split(pair), both, NN)

        @pl.when(core == 0)
        def _():
            text_back(chunk).start()

        @pl.when(core == 1)
        def _():
            image_back_start(chunk)

        turned = split(pair.T)
        visit_grad[early] += dot3((turned[0][rows:], turned[1][rows:]), part, NN)
        grad[early] += dot3((turned[0][:rows], turned[1][:rows]), part, NN)
        return carry

    lax.fori_loop(0, CHUNKS, late_chunk, 0)

    @pl.when(core == 1)
    def _():
        relay_back_step()

    @pl.when(core == 0)
    def _():
        for chunk in range(CHUNKS):
            image_back_start(chunk)

    @pl.when(core == 1)
    def _():
        for chunk in range(CHUNKS):
            text_back(chunk).start()

    store = pltpu.make_async_copy(grad, grad_out, store_sem)
    store.start()

    @pl.when(core == 0)
    def _():
        relay_back_step()

    for which in range(2):
        for chunk in range(CHUNKS):
            pltpu.make_async_copy(
                back_out.at[which, piece(chunk)], back_out.at[which, piece(chunk)],
                back_recv.at[which, chunk],
            ).wait()

    @pl.when(core == 1)
    def _():
        for chunk in range(CHUNKS):
            image_direct(chunk).wait_send()

    for chunk in range(CHUNKS):
        text_copy(chunk).wait_send()
        text_back(chunk).wait_send()
        image_back_direct(chunk).wait_send()
    for copy in meta_copies:
        copy.wait_send()

    @pl.when(x < RUN - 1)
    def _():
        relay_out_copy().wait_send()

    @pl.when(x > 0)
    def _():
        relay_back_copy().wait_send()

    store.wait()


def body(images, texts, image_cluster, text_cluster, text_pair, logit_scale, logit_bias):
    rows, width = images.shape
    step = rows // CHUNKS
    dp_count, inner_count = lax.axis_size("dp"), lax.axis_size("inner")
    dma = pltpu.SemaphoreType.DMA
    f32, bf16 = jnp.float32, jnp.bfloat16
    hbm, free, smem = (
        pl.BlockSpec(memory_space=space) for space in (pltpu.HBM, pl.ANY, pltpu.SMEM)
    )
    grads = jax.ShapeDtypeStruct((2, rows, width), f32)
    held = lambda value: pltpu.with_memory_space_constraint(value, pltpu.HBM)
    own, back = pl.pallas_call(
        functools.partial(kernel, dp_count, inner_count),
        out_shape=(grads, grads),
        in_specs=[hbm] * 5 + [smem] * 2,
        out_specs=(free, free),
        scratch_shapes=[
            pltpu.VMEM((2, rows, width), f32),
            pltpu.VMEM((3, 1, rows), jnp.int32),
            pltpu.VMEM((2, rows, width), f32),
            pltpu.VMEM((2, 2 * rows, width), bf16),
            pltpu.VMEM((2, 2 * rows, width), bf16),
            pltpu.VMEM((2, rows, width), f32),
            pltpu.VMEM((2, rows, width), f32),
            pltpu.VMEM((2, 8, rows), f32),
            pltpu.VMEM((2, 8, rows), f32),
            pltpu.VMEM((2, rows, 8), f32),
            pltpu.VMEM((step, width), f32),
            pltpu.VMEM((step, width), f32),
            dma((5,)),
            dma,
            dma((2, CHUNKS)),
            dma((2, CHUNKS)),
            dma((2,)),
            dma((2,)),
            dma((2, CHUNKS)),
            dma((2, CHUNKS)),
            dma((2,)),
            dma((2,)),
            pltpu.SemaphoreType.REGULAR,
        ],
        compiler_params=pltpu.CompilerParams(
            collective_id=0, has_side_effects=True, vmem_limit_bytes=32 * 1024 * 1024
        ),
        cost_estimate=pl.CostEstimate(
            flops=24 * rows * rows * width, bytes_accessed=24 * rows * width, transcendentals=0
        ),
    )(
        held(images), held(texts),
        held(image_cluster.reshape(1, rows)),
        held(text_cluster.reshape(1, rows)),
        held(text_pair.reshape(1, rows)),
        logit_scale.reshape(1), logit_bias.reshape(1),
    )
    return (own[0] + back[0], own[1] + back[1])


def solution(mesh):
    return jax.shard_map(
        body,
        mesh=mesh,
        in_specs=(
            P(("dp", "inner"), None),
            P(("dp", "inner"), None),
            P(("dp", "inner")),
            P(("dp", "inner")),
            P(("dp", "inner")),
            P(),
            P(),
        ),
        out_specs=(P(("dp", "inner"), None), P(("dp", "inner"), None)),
        check_vma=False,
    )
```

```python
import functools

import jax
import jax.numpy as jnp
from jax import lax
from jax.experimental import pallas as pl
from jax.experimental.pallas import tpu as pltpu
from jax.sharding import PartitionSpec as P

MESH = pl.DeviceIdType.MESH
CHUNKS = 4
RUN = 4


def split(value):
    high = value.astype(jnp.bfloat16)
    low = (value - high.astype(jnp.float32)).astype(jnp.bfloat16)
    return high, low


def dot(left, right, dims):
    return lax.dot_general(left, right, (dims, ((), ())), preferred_element_type=jnp.float32)


def dot3(left, right, dims):
    return (
        dot(left[0], right[0], dims)
        + dot(left[0], right[1], dims)
        + dot(left[1], right[0], dims)
    )


NT = ((1,), (1,))
NN = ((1,), (0,))


def kernel(
    dp_count, inner_count,
    img, txt, img_cluster_in, txt_cluster_in, txt_pair_in, scale_ref, bias_ref,
    grad_out, back_out,
    home, ids, visit, high, low, grad, visit_grad, meta, visit_meta, column,
    relay_out, relay_back,
    load_sem, store_sem, fwd_send, fwd_recv, meta_send, meta_recv,
    back_send, back_recv, relay_send, relay_recv, go_sem,
):
    rows, width = img.shape
    step = rows // CHUNKS
    a, k = lax.axis_index("dp"), lax.axis_index("inner")
    x = a % RUN
    run = a - x
    core = k % 2
    dp_next, dp_prev = (a + 1) % dp_count, (a + dp_count - 1) % dp_count
    in_next, in_prev = (k + 1) % inner_count, (k + inner_count - 1) % inner_count
    run_next, run_prev = (run + RUN) % dp_count, (run + dp_count - 1) % dp_count
    early, late = core, 1 - core
    scale, bias = scale_ref[0], bias_ref[0]

    loads = [
        pltpu.make_async_copy(img, home.at[0], load_sem.at[0]),
        pltpu.make_async_copy(txt, home.at[1], load_sem.at[1]),
        pltpu.make_async_copy(img_cluster_in, ids.at[0], load_sem.at[2]),
        pltpu.make_async_copy(txt_cluster_in, ids.at[1], load_sem.at[3]),
        pltpu.make_async_copy(txt_pair_in, ids.at[2], load_sem.at[4]),
    ]
    for load in loads:
        load.start()

    barrier = pltpu.get_barrier_semaphore()

    def greet(dp, inner):
        pl.semaphore_signal(barrier, inc=1, device_id=(dp, inner), device_id_type=MESH)

    for other in range(1, RUN):
        greet(run + (x + other) % RUN, k)
    greet(a, in_next)
    greet(a, in_prev)
    greet(run_next, k)
    greet(run_prev, k)

    @pl.when(x == 0)
    def _():
        for other in range(2, RUN + 1):
            greet((run + dp_count - other) % dp_count, k)

    @pl.when(x == RUN - 1)
    def _():
        for other in range(1, RUN):
            greet((run + RUN + other) % dp_count, k)

    row = lax.broadcasted_iota(jnp.int32, (8, rows), 0)
    number = (a * inner_count + k) * rows + lax.broadcasted_iota(jnp.int32, (8, rows), 1)
    for load in loads[2:]:
        load.wait()
    wide = lambda slot: jnp.broadcast_to(ids[slot], (8, rows))
    meta[0] = jnp.where(row == 0, number, wide(0)).astype(jnp.float32)
    meta[1] = jnp.where(row == 0, wide(2), wide(1)).astype(jnp.float32)

    end = (x == 0) | (x == RUN - 1)
    pl.semaphore_wait(barrier, jnp.where(end, 2 * RUN + 2, RUN + 3))

    def piece(chunk):
        return pl.ds(pl.multiple_of(chunk * step, step), step)

    def remote(src, dst, send, recv, dp, inner):
        return pltpu.make_async_remote_copy(
            src_ref=src, dst_ref=dst, send_sem=send, recv_sem=recv,
            device_id=(dp, inner), device_id_type=MESH,
        )

    meta_copies = [
        remote(meta.at[0], visit_meta.at[0], meta_send.at[0], meta_recv.at[0], dp_next, k),
        remote(meta.at[1], visit_meta.at[1], meta_send.at[1], meta_recv.at[1], a, in_next),
    ]

    def image_direct(chunk):
        return remote(
            img.at[piece(chunk)], visit.at[0, piece(chunk)],
            fwd_send.at[0, chunk], fwd_recv.at[0, chunk], dp_next, k,
        )

    def image_start(chunk):
        if chunk == 0:
            image_direct(chunk).start()
            return

        @pl.when(x < RUN - 1)
        def _():
            image_direct(chunk).start()

        @pl.when(x == RUN - 1)
        def _():
            remote(
                img.at[piece(chunk)], relay_out,
                fwd_send.at[0, chunk], relay_recv.at[0], run + chunk - 1, k,
            ).start()

    def text_copy(chunk):
        return remote(
            txt.at[piece(chunk)], visit.at[1, piece(chunk)],
            fwd_send.at[1, chunk], fwd_recv.at[1, chunk], a, in_next,
        )

    def relay_out_copy():
        chunk = (x + 1) % CHUNKS
        return remote(
            relay_out, visit.at[0, piece(chunk)],
            relay_send.at[0], fwd_recv.at[0, chunk], run_next, k,
        )

    def relay_out_step():
        @pl.when(x < RUN - 1)
        def _():
            remote(relay_out, relay_out, relay_send.at[0], relay_recv.at[0], run_next, k).wait_recv()
            relay_out_copy().start()

    def image_back_direct(chunk):
        return remote(
            visit_grad.at[0, piece(chunk)], back_out.at[0, piece(chunk)],
            back_send.at[0, chunk], back_recv.at[0, chunk], dp_prev, k,
        )

    def image_back_start(chunk):
        aside = (x == 0) & (chunk > 0)

        @pl.when(jnp.logical_not(aside))
        def _():
            image_back_direct(chunk).start()

        @pl.when(aside)
        def _():
            remote(
                visit_grad.at[0, piece(chunk)], relay_back,
                back_send.at[0, chunk], relay_recv.at[1], run + chunk, k,
            ).start()

    def relay_back_copy():
        return remote(
            relay_back, back_out.at[0, piece(x)],
            relay_send.at[1], back_recv.at[0, x], run_prev, k,
        )

    def relay_back_step():
        @pl.when(x > 0)
        def _():
            remote(relay_back, relay_back, relay_send.at[1], relay_recv.at[1], run_prev, k).wait_recv()
            relay_back_copy().start()

    def text_back(chunk):
        return remote(
            visit_grad.at[1, piece(chunk)], back_out.at[1, piece(chunk)],
            back_send.at[1, chunk], back_recv.at[1, chunk], a, in_prev,
        )

    def fwd_wait(which, chunk):
        pltpu.make_async_copy(
            visit.at[which, piece(chunk)], visit.at[which, piece(chunk)], fwd_recv.at[which, chunk]
        ).wait()

    def weights(logits, left, right):
        logits = scale * logits + bias
        positive = left[:, 0:1] == right[0:1, :]
        other = left[:, 1:2] != right[1:2, :]
        sig = jax.nn.sigmoid(jnp.where(positive, -logits, logits))
        return scale * jnp.where(positive, -sig, jnp.where(other, sig, 0.0))

    for copy in meta_copies:
        copy.start()

    @pl.when((core == 0) | (x == RUN - 1))
    def _():
        for chunk in range(CHUNKS):
            image_start(chunk)

    text_copy(0).start()

    @pl.when(core == 0)
    def _():
        for chunk in range(1, CHUNKS):
            text_copy(chunk).start()

    near, far = pl.ds(0, rows), pl.ds(rows, rows)
    for which in range(2):
        loads[which].wait()
        high[which, near], low[which, near] = split(home[which])
    early_near = (high[early, near], low[early, near])
    late_near = (high[late, near], low[late, near])
    column[0] = jnp.transpose(meta[late])
    pair = weights(dot3(late_near, early_near, NT), column[0], meta[early])
    grad[late] = dot3(split(pair), early_near, NN)
    grad[early] = dot3(split(pair.T), late_near, NN)

    @pl.when(core == 0)
    def _():
        relay_out_step()

        @pl.when(x < RUN - 1)
        def _():
            relay_out_copy().wait_send()

        image_direct(0).wait_send()
        pl.semaphore_signal(go_sem.at[0], inc=1, device_id=(a, in_next), device_id_type=MESH)
        for chunk in range(1, CHUNKS):
            image_direct(chunk).wait_send()

        @pl.when(x < RUN - 1)
        def _():
            pl.semaphore_signal(go_sem.at[1], inc=1, device_id=(a, in_next), device_id_type=MESH)

    pltpu.make_async_copy(visit_meta.at[early], visit_meta.at[early], meta_recv.at[early]).wait()
    for chunk in range(CHUNKS):
        fwd_wait(early, chunk)
    high[early, far], low[early, far] = split(visit[early])
    early_far = (high[early, far], low[early, far])
    late_near = (high[late, near], low[late, near])
    pair = weights(dot3(late_near, early_far, NT), column[0], visit_meta[early])
    grad[late] += dot3(split(pair), early_far, NN)
    visit_grad[early] = dot3(split(pair.T), late_near, NN)

    @pl.when(core == 1)
    def _():
        pl.semaphore_wait(go_sem.at[0], 1)
        for chunk in range(1, CHUNKS):
            text_copy(chunk).start()
        relay_out_step()

        @pl.when(x < RUN - 1)
        def _():
            pl.semaphore_wait(go_sem.at[1], 1)
            for chunk in range(CHUNKS):
                image_direct(chunk).start()

    pltpu.make_async_copy(visit_meta.at[late], visit_meta.at[late], meta_recv.at[late]).wait()
    column[1] = jnp.transpose(visit_meta[late])

    def late_chunk(chunk, carry):
        fwd_wait(late, chunk)
        here = piece(chunk)
        part = split(visit[late, here])
        both = (high[early], low[early])
        right = jnp.concatenate([meta[early], visit_meta[early]], axis=1)
        pair = weights(dot3(part, both, NT), column[1, here], right)
        visit_grad[late, here] = dot3(split(pair), both, NN)

        @pl.when(core == 0)
        def _():
            text_back(chunk).start()

        @pl.when(core == 1)
        def _():
            image_back_start(chunk)

        turned = split(pair.T)
        visit_grad[early] += dot3((turned[0][rows:], turned[1][rows:]), part, NN)
        grad[early] += dot3((turned[0][:rows], turned[1][:rows]), part, NN)
        return carry

    lax.fori_loop(0, CHUNKS, late_chunk, 0)

    @pl.when(core == 1)
    def _():
        relay_back_step()

    @pl.when(core == 0)
    def _():
        for chunk in range(CHUNKS):
            image_back_start(chunk)

    @pl.when(core == 1)
    def _():
        for chunk in range(CHUNKS):
            text_back(chunk).start()

    store = pltpu.make_async_copy(grad, grad_out, store_sem)
    store.start()

    @pl.when(core == 0)
    def _():
        relay_back_step()

    for which in range(2):
        for chunk in range(CHUNKS):
            pltpu.make_async_copy(
                back_out.at[which, piece(chunk)], back_out.at[which, piece(chunk)],
                back_recv.at[which, chunk],
            ).wait()

    @pl.when(core == 1)
    def _():
        for chunk in range(CHUNKS):
            image_direct(chunk).wait_send()

    for chunk in range(CHUNKS):
        text_copy(chunk).wait_send()
        text_back(chunk).wait_send()
        image_back_direct(chunk).wait_send()
    for copy in meta_copies:
        copy.wait_send()

    @pl.when((core == 1) & (x < RUN - 1))
    def _():
        relay_out_copy().wait_send()

    @pl.when(x > 0)
    def _():
        relay_back_copy().wait_send()

    store.wait()


def body(images, texts, image_cluster, text_cluster, text_pair, logit_scale, logit_bias):
    rows, width = images.shape
    step = rows // CHUNKS
    dp_count, inner_count = lax.axis_size("dp"), lax.axis_size("inner")
    dma = pltpu.SemaphoreType.DMA
    f32, bf16 = jnp.float32, jnp.bfloat16
    hbm, free, smem = (
        pl.BlockSpec(memory_space=space) for space in (pltpu.HBM, pl.ANY, pltpu.SMEM)
    )
    grads = jax.ShapeDtypeStruct((2, rows, width), f32)
    held = lambda value: pltpu.with_memory_space_constraint(value, pltpu.HBM)
    own, back = pl.pallas_call(
        functools.partial(kernel, dp_count, inner_count),
        out_shape=(grads, grads),
        in_specs=[hbm] * 5 + [smem] * 2,
        out_specs=(free, free),
        scratch_shapes=[
            pltpu.VMEM((2, rows, width), f32),
            pltpu.VMEM((3, 1, rows), jnp.int32),
            pltpu.VMEM((2, rows, width), f32),
            pltpu.VMEM((2, 2 * rows, width), bf16),
            pltpu.VMEM((2, 2 * rows, width), bf16),
            pltpu.VMEM((2, rows, width), f32),
            pltpu.VMEM((2, rows, width), f32),
            pltpu.VMEM((2, 8, rows), f32),
            pltpu.VMEM((2, 8, rows), f32),
            pltpu.VMEM((2, rows, 8), f32),
            pltpu.VMEM((step, width), f32),
            pltpu.VMEM((step, width), f32),
            dma((5,)),
            dma,
            dma((2, CHUNKS)),
            dma((2, CHUNKS)),
            dma((2,)),
            dma((2,)),
            dma((2, CHUNKS)),
            dma((2, CHUNKS)),
            dma((2,)),
            dma((2,)),
            pltpu.SemaphoreType.REGULAR((2,)),
        ],
        compiler_params=pltpu.CompilerParams(
            collective_id=0, has_side_effects=True, vmem_limit_bytes=32 * 1024 * 1024
        ),
        cost_estimate=pl.CostEstimate(
            flops=24 * rows * rows * width, bytes_accessed=24 * rows * width, transcendentals=0
        ),
    )(
        held(images), held(texts),
        held(image_cluster.reshape(1, rows)),
        held(text_cluster.reshape(1, rows)),
        held(text_pair.reshape(1, rows)),
        logit_scale.reshape(1), logit_bias.reshape(1),
    )
    return (own[0] + back[0], own[1] + back[1])


def solution(mesh):
    return jax.shard_map(
        body,
        mesh=mesh,
        in_specs=(
            P(("dp", "inner"), None),
            P(("dp", "inner"), None),
            P(("dp", "inner")),
            P(("dp", "inner")),
            P(("dp", "inner")),
            P(),
            P(),
        ),
        out_specs=(P(("dp", "inner"), None), P(("dp", "inner"), None)),
        check_vma=False,
    )
```

```python
import functools

import jax
import jax.numpy as jnp
from jax import lax
from jax.experimental import pallas as pl
from jax.experimental.pallas import tpu as pltpu
from jax.sharding import PartitionSpec as P

MESH = pl.DeviceIdType.MESH
CHUNKS = 4
RUN = 4


def split(value):
    high = value.astype(jnp.bfloat16)
    low = (value - high.astype(jnp.float32)).astype(jnp.bfloat16)
    return high, low


def dot(left, right, dims):
    return lax.dot_general(left, right, (dims, ((), ())), preferred_element_type=jnp.float32)


def dot3(left, right, dims):
    return (
        dot(left[0], right[0], dims)
        + dot(left[0], right[1], dims)
        + dot(left[1], right[0], dims)
    )


NT = ((1,), (1,))
NN = ((1,), (0,))


def kernel(
    dp_count, inner_count,
    img, txt, img_cluster_in, txt_cluster_in, txt_pair_in, scale_ref, bias_ref,
    grad_out, back_out,
    home, ids, visit, high, low, grad, visit_grad, meta, visit_meta, column,
    relay_out, relay_back,
    load_sem, store_sem, fwd_send, fwd_recv, meta_send, meta_recv,
    back_send, back_recv, relay_send, relay_recv, go_sem,
):
    rows, width = img.shape
    step = rows // CHUNKS
    a, k = lax.axis_index("dp"), lax.axis_index("inner")
    x = a % RUN
    run = a - x
    core = k % 2
    dp_next, dp_prev = (a + 1) % dp_count, (a + dp_count - 1) % dp_count
    in_next, in_prev = (k + 1) % inner_count, (k + inner_count - 1) % inner_count
    run_next, run_prev = (run + RUN) % dp_count, (run + dp_count - 1) % dp_count
    early, late = core, 1 - core
    scale, bias = scale_ref[0], bias_ref[0]

    loads = [
        pltpu.make_async_copy(img, home.at[0], load_sem.at[0]),
        pltpu.make_async_copy(txt, home.at[1], load_sem.at[1]),
        pltpu.make_async_copy(img_cluster_in, ids.at[0], load_sem.at[2]),
        pltpu.make_async_copy(txt_cluster_in, ids.at[1], load_sem.at[3]),
        pltpu.make_async_copy(txt_pair_in, ids.at[2], load_sem.at[4]),
    ]
    for load in loads:
        load.start()

    barrier = pltpu.get_barrier_semaphore()

    def greet(dp, inner):
        pl.semaphore_signal(barrier, inc=1, device_id=(dp, inner), device_id_type=MESH)

    for other in range(1, RUN):
        greet(run + (x + other) % RUN, k)
    greet(a, in_next)
    greet(a, in_prev)
    greet(run_next, k)
    greet(run_prev, k)

    @pl.when(x == 0)
    def _():
        for other in range(2, RUN + 1):
            greet((run + dp_count - other) % dp_count, k)

    @pl.when(x == RUN - 1)
    def _():
        for other in range(1, RUN):
            greet((run + RUN + other) % dp_count, k)

    row = lax.broadcasted_iota(jnp.int32, (8, rows), 0)
    number = (a * inner_count + k) * rows + lax.broadcasted_iota(jnp.int32, (8, rows), 1)
    for load in loads[2:]:
        load.wait()
    wide = lambda slot: jnp.broadcast_to(ids[slot], (8, rows))
    meta[0] = jnp.where(row == 0, number, wide(0)).astype(jnp.float32)
    meta[1] = jnp.where(row == 0, wide(2), wide(1)).astype(jnp.float32)

    end = (x == 0) | (x == RUN - 1)
    pl.semaphore_wait(barrier, jnp.where(end, 2 * RUN + 2, RUN + 3))

    def piece(chunk):
        return pl.ds(pl.multiple_of(chunk * step, step), step)

    def remote(src, dst, send, recv, dp, inner):
        return pltpu.make_async_remote_copy(
            src_ref=src, dst_ref=dst, send_sem=send, recv_sem=recv,
            device_id=(dp, inner), device_id_type=MESH,
        )

    meta_copies = [
        remote(meta.at[0], visit_meta.at[0], meta_send.at[0], meta_recv.at[0], dp_next, k),
        remote(meta.at[1], visit_meta.at[1], meta_send.at[1], meta_recv.at[1], a, in_next),
    ]

    def image_direct(chunk):
        return remote(
            img.at[piece(chunk)], visit.at[0, piece(chunk)],
            fwd_send.at[0, chunk], fwd_recv.at[0, chunk], dp_next, k,
        )

    def image_start(chunk):
        if chunk == CHUNKS - 1:
            image_direct(chunk).start()
            return

        @pl.when(x < RUN - 1)
        def _():
            image_direct(chunk).start()

        @pl.when(x == RUN - 1)
        def _():
            remote(
                img.at[piece(chunk)], relay_out,
                fwd_send.at[0, chunk], relay_recv.at[0], run + chunk, k,
            ).start()

    def text_copy(chunk):
        return remote(
            txt.at[piece(chunk)], visit.at[1, piece(chunk)],
            fwd_send.at[1, chunk], fwd_recv.at[1, chunk], a, in_next,
        )

    def relay_out_copy():
        return remote(
            relay_out, visit.at[0, piece(x)],
            relay_send.at[0], fwd_recv.at[0, x], run_next, k,
        )

    def relay_out_step():
        @pl.when(x < RUN - 1)
        def _():
            remote(relay_out, relay_out, relay_send.at[0], relay_recv.at[0], run_next, k).wait_recv()
            relay_out_copy().start()

    def image_back_direct(chunk):
        return remote(
            visit_grad.at[0, piece(chunk)], back_out.at[0, piece(chunk)],
            back_send.at[0, chunk], back_recv.at[0, chunk], dp_prev, k,
        )

    def image_back_start(chunk):
        aside = (x == 0) & (chunk < CHUNKS - 1)

        @pl.when(jnp.logical_not(aside))
        def _():
            image_back_direct(chunk).start()

        @pl.when(aside)
        def _():
            remote(
                visit_grad.at[0, piece(chunk)], relay_back,
                back_send.at[0, chunk], relay_recv.at[1], run + chunk + 1, k,
            ).start()

    def relay_back_copy():
        chunk = (x + CHUNKS - 1) % CHUNKS
        return remote(
            relay_back, back_out.at[0, piece(chunk)],
            relay_send.at[1], back_recv.at[0, chunk], run_prev, k,
        )

    def relay_back_step():
        @pl.when(x > 0)
        def _():
            remote(relay_back, relay_back, relay_send.at[1], relay_recv.at[1], run_prev, k).wait_recv()
            relay_back_copy().start()

    def text_back(chunk):
        return remote(
            visit_grad.at[1, piece(chunk)], back_out.at[1, piece(chunk)],
            back_send.at[1, chunk], back_recv.at[1, chunk], a, in_prev,
        )

    def fwd_wait(which, chunk):
        pltpu.make_async_copy(
            visit.at[which, piece(chunk)], visit.at[which, piece(chunk)], fwd_recv.at[which, chunk]
        ).wait()

    def weights(logits, left, right):
        logits = scale * logits + bias
        positive = left[:, 0:1] == right[0:1, :]
        other = left[:, 1:2] != right[1:2, :]
        sig = jax.nn.sigmoid(jnp.where(positive, -logits, logits))
        return scale * jnp.where(positive, -sig, jnp.where(other, sig, 0.0))

    for copy in meta_copies:
        copy.start()

    @pl.when(core == 0)
    def _():
        for chunk in range(CHUNKS):
            image_start(chunk)

    for chunk in range(CHUNKS):
        text_copy(chunk).start()

    @pl.when((core == 1) & (x == RUN - 1))
    def _():
        for chunk in range(CHUNKS):
            image_start(chunk)

    near, far = pl.ds(0, rows), pl.ds(rows, rows)
    for which in range(2):
        loads[which].wait()
        high[which, near], low[which, near] = split(home[which])
    early_near = (high[early, near], low[early, near])
    late_near = (high[late, near], low[late, near])
    column[0] = jnp.transpose(meta[late])
    pair = weights(dot3(late_near, early_near, NT), column[0], meta[early])
    grad[late] = dot3(split(pair), early_near, NN)
    grad[early] = dot3(split(pair.T), late_near, NN)

    @pl.when(core == 0)
    def _():
        relay_out_step()
        for chunk in range(CHUNKS):
            image_direct(chunk).wait_send()

        @pl.when(x < RUN - 1)
        def _():
            pl.semaphore_signal(go_sem, inc=1, device_id=(a, in_next), device_id_type=MESH)

    pltpu.make_async_copy(visit_meta.at[early], visit_meta.at[early], meta_recv.at[early]).wait()
    for chunk in range(CHUNKS):
        fwd_wait(early, chunk)
    high[early, far], low[early, far] = split(visit[early])
    early_far = (high[early, far], low[early, far])
    late_near = (high[late, near], low[late, near])
    pair = weights(dot3(late_near, early_far, NT), column[0], visit_meta[early])
    grad[late] += dot3(split(pair), early_far, NN)
    visit_grad[early] = dot3(split(pair.T), late_near, NN)

    @pl.when(core == 1)
    def _():
        @pl.when(x < RUN - 1)
        def _():
            pl.semaphore_wait(go_sem, 1)
            for chunk in range(CHUNKS):
                image_direct(chunk).start()

        relay_out_step()

    pltpu.make_async_copy(visit_meta.at[late], visit_meta.at[late], meta_recv.at[late]).wait()
    column[1] = jnp.transpose(visit_meta[late])

    def late_chunk(chunk, carry):
        fwd_wait(late, chunk)
        here = piece(chunk)
        part = split(visit[late, here])
        both = (high[early], low[early])
        right = jnp.concatenate([meta[early], visit_meta[early]], axis=1)
        pair = weights(dot3(part, both, NT), column[1, here], right)
        visit_grad[late, here] = dot3(split(pair), both, NN)

        @pl.when(core == 0)
        def _():
            text_back(chunk).start()

        @pl.when(core == 1)
        def _():
            image_back_start(chunk)

        turned = split(pair.T)
        visit_grad[early] += dot3((turned[0][rows:], turned[1][rows:]), part, NN)
        grad[early] += dot3((turned[0][:rows], turned[1][:rows]), part, NN)
        return carry

    lax.fori_loop(0, CHUNKS, late_chunk, 0)

    @pl.when(core == 1)
    def _():
        relay_back_step()

    @pl.when(core == 0)
    def _():
        for chunk in range(CHUNKS):
            image_back_start(chunk)

    @pl.when(core == 1)
    def _():
        for chunk in range(CHUNKS):
            text_back(chunk).start()

    store = pltpu.make_async_copy(grad, grad_out, store_sem)
    store.start()

    @pl.when(core == 0)
    def _():
        relay_back_step()

    for which in range(2):
        for chunk in range(CHUNKS):
            pltpu.make_async_copy(
                back_out.at[which, piece(chunk)], back_out.at[which, piece(chunk)],
                back_recv.at[which, chunk],
            ).wait()

    @pl.when(core == 1)
    def _():
        for chunk in range(CHUNKS):
            image_direct(chunk).wait_send()

    for chunk in range(CHUNKS):
        text_copy(chunk).wait_send()
        text_back(chunk).wait_send()
        image_back_direct(chunk).wait_send()
    for copy in meta_copies:
        copy.wait_send()

    @pl.when(x < RUN - 1)
    def _():
        relay_out_copy().wait_send()

    @pl.when(x > 0)
    def _():
        relay_back_copy().wait_send()

    store.wait()


def body(images, texts, image_cluster, text_cluster, text_pair, logit_scale, logit_bias):
    rows, width = images.shape
    step = rows // CHUNKS
    dp_count, inner_count = lax.axis_size("dp"), lax.axis_size("inner")
    dma = pltpu.SemaphoreType.DMA
    f32, bf16 = jnp.float32, jnp.bfloat16
    hbm, free, smem = (
        pl.BlockSpec(memory_space=space) for space in (pltpu.HBM, pl.ANY, pltpu.SMEM)
    )
    grads = jax.ShapeDtypeStruct((2, rows, width), f32)
    held = lambda value: pltpu.with_memory_space_constraint(value, pltpu.HBM)
    own, back = pl.pallas_call(
        functools.partial(kernel, dp_count, inner_count),
        out_shape=(grads, grads),
        in_specs=[hbm] * 5 + [smem] * 2,
        out_specs=(free, free),
        scratch_shapes=[
            pltpu.VMEM((2, rows, width), f32),
            pltpu.VMEM((3, 1, rows), jnp.int32),
            pltpu.VMEM((2, rows, width), f32),
            pltpu.VMEM((2, 2 * rows, width), bf16),
            pltpu.VMEM((2, 2 * rows, width), bf16),
            pltpu.VMEM((2, rows, width), f32),
            pltpu.VMEM((2, rows, width), f32),
            pltpu.VMEM((2, 8, rows), f32),
            pltpu.VMEM((2, 8, rows), f32),
            pltpu.VMEM((2, rows, 8), f32),
            pltpu.VMEM((step, width), f32),
            pltpu.VMEM((step, width), f32),
            dma((5,)),
            dma,
            dma((2, CHUNKS)),
            dma((2, CHUNKS)),
            dma((2,)),
            dma((2,)),
            dma((2, CHUNKS)),
            dma((2, CHUNKS)),
            dma((2,)),
            dma((2,)),
            pltpu.SemaphoreType.REGULAR,
        ],
        compiler_params=pltpu.CompilerParams(
            collective_id=0, has_side_effects=True, vmem_limit_bytes=32 * 1024 * 1024
        ),
        cost_estimate=pl.CostEstimate(
            flops=24 * rows * rows * width, bytes_accessed=24 * rows * width, transcendentals=0
        ),
    )(
        held(images), held(texts),
        held(image_cluster.reshape(1, rows)),
        held(text_cluster.reshape(1, rows)),
        held(text_pair.reshape(1, rows)),
        logit_scale.reshape(1), logit_bias.reshape(1),
    )
    return (own[0] + back[0], own[1] + back[1])


def solution(mesh):
    return jax.shard_map(
        body,
        mesh=mesh,
        in_specs=(
            P(("dp", "inner"), None),
            P(("dp", "inner"), None),
            P(("dp", "inner")),
            P(("dp", "inner")),
            P(("dp", "inner")),
            P(),
            P(),
        ),
        out_specs=(P(("dp", "inner"), None), P(("dp", "inner"), None)),
        check_vma=False,
    )
```

```python
import functools

import jax
import jax.numpy as jnp
from jax import lax
from jax.experimental import pallas as pl
from jax.experimental.pallas import tpu as pltpu
from jax.sharding import PartitionSpec as P

MESH = pl.DeviceIdType.MESH
CHUNKS = 4
RUN = 4


def split(value):
    high = value.astype(jnp.bfloat16)
    low = (value - high.astype(jnp.float32)).astype(jnp.bfloat16)
    return high, low


def dot(left, right, dims):
    return lax.dot_general(left, right, (dims, ((), ())), preferred_element_type=jnp.float32)


def dot3(left, right, dims):
    return (
        dot(left[0], right[0], dims)
        + dot(left[0], right[1], dims)
        + dot(left[1], right[0], dims)
    )


NT = ((1,), (1,))
NN = ((1,), (0,))


def kernel(
    dp_count, inner_count,
    img, txt, img_cluster_in, txt_cluster_in, txt_pair_in, scale_ref, bias_ref,
    grad_out, back_out,
    home, ids, visit, high, low, grad, visit_grad, meta, visit_meta, column,
    relay_out, relay_back,
    load_sem, store_sem, fwd_send, fwd_recv, meta_send, meta_recv,
    back_send, back_recv, relay_send, relay_recv, go_sem,
):
    rows, width = img.shape
    step = rows // CHUNKS
    a, k = lax.axis_index("dp"), lax.axis_index("inner")
    x = a % RUN
    run = a - x
    core = k % 2
    dp_next, dp_prev = (a + 1) % dp_count, (a + dp_count - 1) % dp_count
    in_next, in_prev = (k + 1) % inner_count, (k + inner_count - 1) % inner_count
    run_next, run_prev = (run + RUN) % dp_count, (run + dp_count - 1) % dp_count
    early, late = core, 1 - core
    scale, bias = scale_ref[0], bias_ref[0]

    loads = [
        pltpu.make_async_copy(img, home.at[0], load_sem.at[0]),
        pltpu.make_async_copy(txt, home.at[1], load_sem.at[1]),
        pltpu.make_async_copy(img_cluster_in, ids.at[0], load_sem.at[2]),
        pltpu.make_async_copy(txt_cluster_in, ids.at[1], load_sem.at[3]),
        pltpu.make_async_copy(txt_pair_in, ids.at[2], load_sem.at[4]),
    ]
    for load in loads:
        load.start()

    barrier = pltpu.get_barrier_semaphore()

    def greet(dp, inner):
        pl.semaphore_signal(barrier, inc=1, device_id=(dp, inner), device_id_type=MESH)

    for other in range(1, RUN):
        greet(run + (x + other) % RUN, k)
    greet(a, in_next)
    greet(a, in_prev)
    greet(run_next, k)
    greet(run_prev, k)

    @pl.when(x == 0)
    def _():
        for other in range(2, RUN + 1):
            greet((run + dp_count - other) % dp_count, k)

    @pl.when(x == RUN - 1)
    def _():
        for other in range(1, RUN):
            greet((run + RUN + other) % dp_count, k)

    row = lax.broadcasted_iota(jnp.int32, (8, rows), 0)
    number = (a * inner_count + k) * rows + lax.broadcasted_iota(jnp.int32, (8, rows), 1)
    for load in loads[2:]:
        load.wait()
    wide = lambda slot: jnp.broadcast_to(ids[slot], (8, rows))
    meta[0] = jnp.where(row == 0, number, wide(0)).astype(jnp.float32)
    meta[1] = jnp.where(row == 0, wide(2), wide(1)).astype(jnp.float32)

    end = (x == 0) | (x == RUN - 1)
    pl.semaphore_wait(barrier, jnp.where(end, 2 * RUN + 2, RUN + 3))

    def piece(chunk):
        return pl.ds(pl.multiple_of(chunk * step, step), step)

    def remote(src, dst, send, recv, dp, inner):
        return pltpu.make_async_remote_copy(
            src_ref=src, dst_ref=dst, send_sem=send, recv_sem=recv,
            device_id=(dp, inner), device_id_type=MESH,
        )

    meta_copies = [
        remote(meta.at[0], visit_meta.at[0], meta_send.at[0], meta_recv.at[0], dp_next, k),
        remote(meta.at[1], visit_meta.at[1], meta_send.at[1], meta_recv.at[1], a, in_next),
    ]

    def image_direct(chunk):
        return remote(
            img.at[piece(chunk)], visit.at[0, piece(chunk)],
            fwd_send.at[0, chunk], fwd_recv.at[0, chunk], dp_next, k,
        )

    def image_start(chunk):
        if chunk == CHUNKS - 1:
            image_direct(chunk).start()
            return

        @pl.when(x < RUN - 1)
        def _():
            image_direct(chunk).start()

        @pl.when(x == RUN - 1)
        def _():
            remote(
                img.at[piece(chunk)], relay_out,
                fwd_send.at[0, chunk], relay_recv.at[0], run + chunk, k,
            ).start()

    def text_copy(chunk):
        return remote(
            txt.at[piece(chunk)], visit.at[1, piece(chunk)],
            fwd_send.at[1, chunk], fwd_recv.at[1, chunk], a, in_next,
        )

    def relay_out_copy():
        return remote(
            relay_out, visit.at[0, piece(x)],
            relay_send.at[0], fwd_recv.at[0, x], run_next, k,
        )

    def relay_out_step():
        @pl.when(x < RUN - 1)
        def _():
            remote(relay_out, relay_out, relay_send.at[0], relay_recv.at[0], run_next, k).wait_recv()
            relay_out_copy().start()

    def image_back_direct(chunk):
        return remote(
            visit_grad.at[0, piece(chunk)], back_out.at[0, piece(chunk)],
            back_send.at[0, chunk], back_recv.at[0, chunk], dp_prev, k,
        )

    def image_back_start(chunk):
        aside = (x == 0) & (chunk < CHUNKS - 1)

        @pl.when(jnp.logical_not(aside))
        def _():
            image_back_direct(chunk).start()

        @pl.when(aside)
        def _():
            remote(
                visit_grad.at[0, piece(chunk)], relay_back,
                back_send.at[0, chunk], relay_recv.at[1], run + chunk + 1, k,
            ).start()

    def relay_back_copy():
        chunk = (x + CHUNKS - 1) % CHUNKS
        return remote(
            relay_back, back_out.at[0, piece(chunk)],
            relay_send.at[1], back_recv.at[0, chunk], run_prev, k,
        )

    def relay_back_step():
        @pl.when(x > 0)
        def _():
            remote(relay_back, relay_back, relay_send.at[1], relay_recv.at[1], run_prev, k).wait_recv()
            relay_back_copy().start()

    def text_back(chunk):
        return remote(
            visit_grad.at[1, piece(chunk)], back_out.at[1, piece(chunk)],
            back_send.at[1, chunk], back_recv.at[1, chunk], a, in_prev,
        )

    def fwd_wait(which, chunk):
        pltpu.make_async_copy(
            visit.at[which, piece(chunk)], visit.at[which, piece(chunk)], fwd_recv.at[which, chunk]
        ).wait()

    def weights(logits, left, right):
        logits = scale * logits + bias
        positive = left[:, 0:1] == right[0:1, :]
        other = left[:, 1:2] != right[1:2, :]
        sig = jax.nn.sigmoid(jnp.where(positive, -logits, logits))
        return scale * jnp.where(positive, -sig, jnp.where(other, sig, 0.0))

    for copy in meta_copies:
        copy.start()

    @pl.when(core == 0)
    def _():
        for chunk in range(CHUNKS):
            image_start(chunk)

    for chunk in range(CHUNKS):
        text_copy(chunk).start()

    @pl.when((core == 1) & (x == RUN - 1))
    def _():
        for chunk in range(CHUNKS):
            image_start(chunk)

    near, far = pl.ds(0, rows), pl.ds(rows, rows)
    for which in range(2):
        loads[which].wait()
        high[which, near], low[which, near] = split(home[which])
    early_near = (high[early, near], low[early, near])
    late_near = (high[late, near], low[late, near])
    column[0] = jnp.transpose(meta[late])
    pair = weights(dot3(late_near, early_near, NT), column[0], meta[early])
    grad[late] = dot3(split(pair), early_near, NN)
    grad[early] = dot3(split(pair.T), late_near, NN)

    @pl.when(core == 0)
    def _():
        relay_out_step()
        for chunk in range(CHUNKS):
            image_direct(chunk).wait_send()

        @pl.when(x < RUN - 1)
        def _():
            pl.semaphore_signal(go_sem, inc=1, device_id=(a, in_next), device_id_type=MESH)

    pltpu.make_async_copy(visit_meta.at[early], visit_meta.at[early], meta_recv.at[early]).wait()
    for chunk in range(CHUNKS):
        fwd_wait(early, chunk)
    high[early, far], low[early, far] = split(visit[early])
    early_far = (high[early, far], low[early, far])
    late_near = (high[late, near], low[late, near])
    pair = weights(dot3(late_near, early_far, NT), column[0], visit_meta[early])
    grad[late] += dot3(split(pair), early_far, NN)
    visit_grad[early] = dot3(split(pair.T), late_near, NN)

    @pl.when(core == 1)
    def _():
        @pl.when(x < RUN - 1)
        def _():
            pl.semaphore_wait(go_sem, 1)
            for chunk in range(CHUNKS):
                image_direct(chunk).start()

        relay_out_step()

    pltpu.make_async_copy(visit_meta.at[late], visit_meta.at[late], meta_recv.at[late]).wait()
    column[1] = jnp.transpose(visit_meta[late])

    def late_chunk(chunk, carry):
        fwd_wait(late, chunk)
        here = piece(chunk)
        part = split(visit[late, here])
        both = (high[early], low[early])
        right = jnp.concatenate([meta[early], visit_meta[early]], axis=1)
        pair = weights(dot3(part, both, NT), column[1, here], right)
        visit_grad[late, here] = dot3(split(pair), both, NN)

        @pl.when(core == 0)
        def _():
            text_back(chunk).start()

        @pl.when(core == 1)
        def _():
            image_back_start(chunk)

        turned = split(pair.T)
        visit_grad[early] += dot3((turned[0][rows:], turned[1][rows:]), part, NN)
        grad[early] += dot3((turned[0][:rows], turned[1][:rows]), part, NN)
        return carry

    lax.fori_loop(0, CHUNKS, late_chunk, 0)

    @pl.when(core == 1)
    def _():
        relay_back_step()

    @pl.when(core == 0)
    def _():
        for chunk in range(CHUNKS):
            image_back_direct(chunk).start()

    @pl.when(core == 1)
    def _():
        for chunk in range(CHUNKS):
            text_back(chunk).start()

    store = pltpu.make_async_copy(grad, grad_out, store_sem)
    store.start()

    for which in range(2):
        for chunk in range(CHUNKS):
            pltpu.make_async_copy(
                back_out.at[which, piece(chunk)], back_out.at[which, piece(chunk)],
                back_recv.at[which, chunk],
            ).wait()

    @pl.when(core == 1)
    def _():
        for chunk in range(CHUNKS):
            image_direct(chunk).wait_send()

    for chunk in range(CHUNKS):
        text_copy(chunk).wait_send()
        text_back(chunk).wait_send()
        image_back_direct(chunk).wait_send()
    for copy in meta_copies:
        copy.wait_send()

    @pl.when(x < RUN - 1)
    def _():
        relay_out_copy().wait_send()

    @pl.when((core == 1) & (x > 0))
    def _():
        relay_back_copy().wait_send()

    store.wait()


def body(images, texts, image_cluster, text_cluster, text_pair, logit_scale, logit_bias):
    rows, width = images.shape
    step = rows // CHUNKS
    dp_count, inner_count = lax.axis_size("dp"), lax.axis_size("inner")
    dma = pltpu.SemaphoreType.DMA
    f32, bf16 = jnp.float32, jnp.bfloat16
    hbm, free, smem = (
        pl.BlockSpec(memory_space=space) for space in (pltpu.HBM, pl.ANY, pltpu.SMEM)
    )
    grads = jax.ShapeDtypeStruct((2, rows, width), f32)
    held = lambda value: pltpu.with_memory_space_constraint(value, pltpu.HBM)
    own, back = pl.pallas_call(
        functools.partial(kernel, dp_count, inner_count),
        out_shape=(grads, grads),
        in_specs=[hbm] * 5 + [smem] * 2,
        out_specs=(free, free),
        scratch_shapes=[
            pltpu.VMEM((2, rows, width), f32),
            pltpu.VMEM((3, 1, rows), jnp.int32),
            pltpu.VMEM((2, rows, width), f32),
            pltpu.VMEM((2, 2 * rows, width), bf16),
            pltpu.VMEM((2, 2 * rows, width), bf16),
            pltpu.VMEM((2, rows, width), f32),
            pltpu.VMEM((2, rows, width), f32),
            pltpu.VMEM((2, 8, rows), f32),
            pltpu.VMEM((2, 8, rows), f32),
            pltpu.VMEM((2, rows, 8), f32),
            pltpu.VMEM((step, width), f32),
            pltpu.VMEM((step, width), f32),
            dma((5,)),
            dma,
            dma((2, CHUNKS)),
            dma((2, CHUNKS)),
            dma((2,)),
            dma((2,)),
            dma((2, CHUNKS)),
            dma((2, CHUNKS)),
            dma((2,)),
            dma((2,)),
            pltpu.SemaphoreType.REGULAR,
        ],
        compiler_params=pltpu.CompilerParams(
            collective_id=0, has_side_effects=True, vmem_limit_bytes=32 * 1024 * 1024
        ),
        cost_estimate=pl.CostEstimate(
            flops=24 * rows * rows * width, bytes_accessed=24 * rows * width, transcendentals=0
        ),
    )(
        held(images), held(texts),
        held(image_cluster.reshape(1, rows)),
        held(text_cluster.reshape(1, rows)),
        held(text_pair.reshape(1, rows)),
        logit_scale.reshape(1), logit_bias.reshape(1),
    )
    return (own[0] + back[0], own[1] + back[1])


def solution(mesh):
    return jax.shard_map(
        body,
        mesh=mesh,
        in_specs=(
            P(("dp", "inner"), None),
            P(("dp", "inner"), None),
            P(("dp", "inner")),
            P(("dp", "inner")),
            P(("dp", "inner")),
            P(),
            P(),
        ),
        out_specs=(P(("dp", "inner"), None), P(("dp", "inner"), None)),
        check_vma=False,
    )
```

```python
import functools

import jax
import jax.numpy as jnp
from jax import lax
from jax.experimental import pallas as pl
from jax.experimental.pallas import tpu as pltpu
from jax.sharding import PartitionSpec as P

MESH = pl.DeviceIdType.MESH
CHUNKS = 4
RUN = 4


def split(value):
    high = value.astype(jnp.bfloat16)
    low = (value - high.astype(jnp.float32)).astype(jnp.bfloat16)
    return high, low


def dot(left, right, dims):
    return lax.dot_general(left, right, (dims, ((), ())), preferred_element_type=jnp.float32)


def dot3(left, right, dims):
    return (
        dot(left[0], right[0], dims)
        + dot(left[0], right[1], dims)
        + dot(left[1], right[0], dims)
    )


NT = ((1,), (1,))
NN = ((1,), (0,))


def kernel(
    dp_count, inner_count,
    img, txt, img_cluster_in, txt_cluster_in, txt_pair_in, scale_ref, bias_ref,
    grad_out, back_out,
    home, ids, visit, high, low, grad, visit_grad, meta, visit_meta, column,
    relay_out, relay_back,
    load_sem, store_sem, fwd_send, fwd_recv, meta_send, meta_recv,
    back_send, back_recv, relay_send, relay_recv, go_sem,
):
    rows, width = img.shape
    step = rows // CHUNKS
    a, k = lax.axis_index("dp"), lax.axis_index("inner")
    x = a % RUN
    run = a - x
    core = k % 2
    dp_next, dp_prev = (a + 1) % dp_count, (a + dp_count - 1) % dp_count
    in_next, in_prev = (k + 1) % inner_count, (k + inner_count - 1) % inner_count
    run_next, run_prev = (run + RUN) % dp_count, (run + dp_count - 1) % dp_count
    early, late = core, 1 - core
    scale, bias = scale_ref[0], bias_ref[0]

    loads = [
        pltpu.make_async_copy(img, home.at[0], load_sem.at[0]),
        pltpu.make_async_copy(txt, home.at[1], load_sem.at[1]),
        pltpu.make_async_copy(img_cluster_in, ids.at[0], load_sem.at[2]),
        pltpu.make_async_copy(txt_cluster_in, ids.at[1], load_sem.at[3]),
        pltpu.make_async_copy(txt_pair_in, ids.at[2], load_sem.at[4]),
    ]
    for load in loads:
        load.start()

    barrier = pltpu.get_barrier_semaphore()

    def greet(dp, inner):
        pl.semaphore_signal(barrier, inc=1, device_id=(dp, inner), device_id_type=MESH)

    for other in range(1, RUN):
        greet(run + (x + other) % RUN, k)
    greet(a, in_next)
    greet(a, in_prev)
    greet(run_next, k)
    greet(run_prev, k)

    @pl.when(x == 0)
    def _():
        for other in range(2, RUN + 1):
            greet((run + dp_count - other) % dp_count, k)

    @pl.when(x == RUN - 1)
    def _():
        for other in range(1, RUN):
            greet((run + RUN + other) % dp_count, k)

    row = lax.broadcasted_iota(jnp.int32, (8, rows), 0)
    number = (a * inner_count + k) * rows + lax.broadcasted_iota(jnp.int32, (8, rows), 1)
    for load in loads[2:]:
        load.wait()
    wide = lambda slot: jnp.broadcast_to(ids[slot], (8, rows))
    meta[0] = jnp.where(row == 0, number, wide(0)).astype(jnp.float32)
    meta[1] = jnp.where(row == 0, wide(2), wide(1)).astype(jnp.float32)

    end = (x == 0) | (x == RUN - 1)
    pl.semaphore_wait(barrier, jnp.where(end, 2 * RUN + 2, RUN + 3))

    def piece(chunk):
        return pl.ds(pl.multiple_of(chunk * step, step), step)

    def remote(src, dst, send, recv, dp, inner):
        return pltpu.make_async_remote_copy(
            src_ref=src, dst_ref=dst, send_sem=send, recv_sem=recv,
            device_id=(dp, inner), device_id_type=MESH,
        )

    meta_copies = [
        remote(meta.at[0], visit_meta.at[0], meta_send.at[0], meta_recv.at[0], dp_next, k),
        remote(meta.at[1], visit_meta.at[1], meta_send.at[1], meta_recv.at[1], a, in_next),
    ]

    def image_direct(chunk):
        return remote(
            img.at[piece(chunk)], visit.at[0, piece(chunk)],
            fwd_send.at[0, chunk], fwd_recv.at[0, chunk], dp_next, k,
        )

    def image_start(chunk):
        if chunk == CHUNKS - 1:
            image_direct(chunk).start()
            return

        @pl.when(x < RUN - 1)
        def _():
            image_direct(chunk).start()

        @pl.when(x == RUN - 1)
        def _():
            remote(
                img.at[piece(chunk)], relay_out,
                fwd_send.at[0, chunk], relay_recv.at[0], run + chunk, k,
            ).start()

    def text_copy(chunk):
        return remote(
            txt.at[piece(chunk)], visit.at[1, piece(chunk)],
            fwd_send.at[1, chunk], fwd_recv.at[1, chunk], a, in_next,
        )

    def relay_out_copy():
        return remote(
            relay_out, visit.at[0, piece(x)],
            relay_send.at[0], fwd_recv.at[0, x], run_next, k,
        )

    def relay_out_step():
        @pl.when(x < RUN - 1)
        def _():
            remote(relay_out, relay_out, relay_send.at[0], relay_recv.at[0], run_next, k).wait_recv()
            relay_out_copy().start()

    def image_back_direct(chunk):
        return remote(
            visit_grad.at[0, piece(chunk)], back_out.at[0, piece(chunk)],
            back_send.at[0, chunk], back_recv.at[0, chunk], dp_prev, k,
        )

    def image_back_start(chunk):
        aside = (x == 0) & (chunk < CHUNKS - 1)

        @pl.when(jnp.logical_not(aside))
        def _():
            image_back_direct(chunk).start()

        @pl.when(aside)
        def _():
            remote(
                visit_grad.at[0, piece(chunk)], relay_back,
                back_send.at[0, chunk], relay_recv.at[1], run + chunk + 1, k,
            ).start()

    def relay_back_copy():
        chunk = (x + CHUNKS - 1) % CHUNKS
        return remote(
            relay_back, back_out.at[0, piece(chunk)],
            relay_send.at[1], back_recv.at[0, chunk], run_prev, k,
        )

    def relay_back_step():
        @pl.when(x > 0)
        def _():
            remote(relay_back, relay_back, relay_send.at[1], relay_recv.at[1], run_prev, k).wait_recv()
            relay_back_copy().start()

    def text_back(chunk):
        return remote(
            visit_grad.at[1, piece(chunk)], back_out.at[1, piece(chunk)],
            back_send.at[1, chunk], back_recv.at[1, chunk], a, in_prev,
        )

    def fwd_wait(which, chunk):
        pltpu.make_async_copy(
            visit.at[which, piece(chunk)], visit.at[which, piece(chunk)], fwd_recv.at[which, chunk]
        ).wait()

    def weights(logits, left, right):
        logits = scale * logits + bias
        positive = left[:, 0:1] == right[0:1, :]
        other = left[:, 1:2] != right[1:2, :]
        sig = jax.nn.sigmoid(jnp.where(positive, -logits, logits))
        return scale * jnp.where(positive, -sig, jnp.where(other, sig, 0.0))

    for copy in meta_copies:
        copy.start()

    @pl.when(core == 0)
    def _():
        for chunk in range(CHUNKS):
            image_start(chunk)

    for chunk in range(CHUNKS):
        text_copy(chunk).start()

    @pl.when((core == 1) & (x == RUN - 1))
    def _():
        for chunk in range(CHUNKS):
            image_start(chunk)

    near, far = pl.ds(0, rows), pl.ds(rows, rows)
    for which in range(2):
        loads[which].wait()
        high[which, near], low[which, near] = split(home[which])
    early_near = (high[early, near], low[early, near])
    late_near = (high[late, near], low[late, near])
    column[0] = jnp.transpose(meta[late])
    pair = weights(dot3(late_near, early_near, NT), column[0], meta[early])
    grad[late] = dot3(split(pair), early_near, NN)
    grad[early] = dot3(split(pair.T), late_near, NN)

    @pl.when(core == 0)
    def _():
        relay_out_step()
        for chunk in range(CHUNKS):
            image_direct(chunk).wait_send()

        @pl.when(x < RUN - 1)
        def _():
            pl.semaphore_signal(go_sem, inc=1, device_id=(a, in_next), device_id_type=MESH)

    pltpu.make_async_copy(visit_meta.at[early], visit_meta.at[early], meta_recv.at[early]).wait()
    for chunk in range(CHUNKS):
        fwd_wait(early, chunk)
    high[early, far], low[early, far] = split(visit[early])
    early_far = (high[early, far], low[early, far])
    late_near = (high[late, near], low[late, near])
    pair = weights(dot3(late_near, early_far, NT), column[0], visit_meta[early])
    grad[late] += dot3(split(pair), early_far, NN)
    visit_grad[early] = dot3(split(pair.T), late_near, NN)

    @pl.when(core == 1)
    def _():
        @pl.when(x < RUN - 1)
        def _():
            pl.semaphore_wait(go_sem, 1)
            for chunk in range(CHUNKS):
                image_direct(chunk).start()

        relay_out_step()

    pltpu.make_async_copy(visit_meta.at[late], visit_meta.at[late], meta_recv.at[late]).wait()
    column[1] = jnp.transpose(visit_meta[late])

    def late_chunk(chunk, carry):
        fwd_wait(late, chunk)
        here = piece(chunk)
        part = split(visit[late, here])
        both = (high[early], low[early])
        right = jnp.concatenate([meta[early], visit_meta[early]], axis=1)
        pair = weights(dot3(part, both, NT), column[1, here], right)
        visit_grad[late, here] = dot3(split(pair), both, NN)

        @pl.when(core == 0)
        def _():
            text_back(chunk).start()

        @pl.when(core == 1)
        def _():
            image_back_start(chunk)

        turned = split(pair.T)
        visit_grad[early] += dot3((turned[0][rows:], turned[1][rows:]), part, NN)
        grad[early] += dot3((turned[0][:rows], turned[1][:rows]), part, NN)
        return carry

    lax.fori_loop(0, CHUNKS, late_chunk, 0)

    @pl.when(core == 1)
    def _():
        relay_back_step()

    @pl.when(core == 0)
    def _():
        for chunk in range(CHUNKS):
            if chunk == CHUNKS // 2:
                relay_back_step()
            image_back_start(chunk)

    @pl.when(core == 1)
    def _():
        for chunk in range(CHUNKS):
            text_back(chunk).start()

    store = pltpu.make_async_copy(grad, grad_out, store_sem)
    store.start()

    for which in range(2):
        for chunk in range(CHUNKS):
            pltpu.make_async_copy(
                back_out.at[which, piece(chunk)], back_out.at[which, piece(chunk)],
                back_recv.at[which, chunk],
            ).wait()

    @pl.when(core == 1)
    def _():
        for chunk in range(CHUNKS):
            image_direct(chunk).wait_send()

    for chunk in range(CHUNKS):
        text_copy(chunk).wait_send()
        text_back(chunk).wait_send()
        image_back_direct(chunk).wait_send()
    for copy in meta_copies:
        copy.wait_send()

    @pl.when(x < RUN - 1)
    def _():
        relay_out_copy().wait_send()

    @pl.when(x > 0)
    def _():
        relay_back_copy().wait_send()

    store.wait()


def body(images, texts, image_cluster, text_cluster, text_pair, logit_scale, logit_bias):
    rows, width = images.shape
    step = rows // CHUNKS
    dp_count, inner_count = lax.axis_size("dp"), lax.axis_size("inner")
    dma = pltpu.SemaphoreType.DMA
    f32, bf16 = jnp.float32, jnp.bfloat16
    hbm, free, smem = (
        pl.BlockSpec(memory_space=space) for space in (pltpu.HBM, pl.ANY, pltpu.SMEM)
    )
    grads = jax.ShapeDtypeStruct((2, rows, width), f32)
    held = lambda value: pltpu.with_memory_space_constraint(value, pltpu.HBM)
    own, back = pl.pallas_call(
        functools.partial(kernel, dp_count, inner_count),
        out_shape=(grads, grads),
        in_specs=[hbm] * 5 + [smem] * 2,
        out_specs=(free, free),
        scratch_shapes=[
            pltpu.VMEM((2, rows, width), f32),
            pltpu.VMEM((3, 1, rows), jnp.int32),
            pltpu.VMEM((2, rows, width), f32),
            pltpu.VMEM((2, 2 * rows, width), bf16),
            pltpu.VMEM((2, 2 * rows, width), bf16),
            pltpu.VMEM((2, rows, width), f32),
            pltpu.VMEM((2, rows, width), f32),
            pltpu.VMEM((2, 8, rows), f32),
            pltpu.VMEM((2, 8, rows), f32),
            pltpu.VMEM((2, rows, 8), f32),
            pltpu.VMEM((step, width), f32),
            pltpu.VMEM((step, width), f32),
            dma((5,)),
            dma,
            dma((2, CHUNKS)),
            dma((2, CHUNKS)),
            dma((2,)),
            dma((2,)),
            dma((2, CHUNKS)),
            dma((2, CHUNKS)),
            dma((2,)),
            dma((2,)),
            pltpu.SemaphoreType.REGULAR,
        ],
        compiler_params=pltpu.CompilerParams(
            collective_id=0, has_side_effects=True, vmem_limit_bytes=32 * 1024 * 1024
        ),
        cost_estimate=pl.CostEstimate(
            flops=24 * rows * rows * width, bytes_accessed=24 * rows * width, transcendentals=0
        ),
    )(
        held(images), held(texts),
        held(image_cluster.reshape(1, rows)),
        held(text_cluster.reshape(1, rows)),
        held(text_pair.reshape(1, rows)),
        logit_scale.reshape(1), logit_bias.reshape(1),
    )
    return (own[0] + back[0], own[1] + back[1])


def solution(mesh):
    return jax.shard_map(
        body,
        mesh=mesh,
        in_specs=(
            P(("dp", "inner"), None),
            P(("dp", "inner"), None),
            P(("dp", "inner")),
            P(("dp", "inner")),
            P(("dp", "inner")),
            P(),
            P(),
        ),
        out_specs=(P(("dp", "inner"), None), P(("dp", "inner"), None)),
        check_vma=False,
    )
```

```python
import functools

import jax
import jax.numpy as jnp
from jax import lax
from jax.experimental import pallas as pl
from jax.experimental.pallas import tpu as pltpu
from jax.sharding import PartitionSpec as P

MESH = pl.DeviceIdType.MESH
CHUNKS = 4
RUN = 4


def split(value):
    high = value.astype(jnp.bfloat16)
    low = (value - high.astype(jnp.float32)).astype(jnp.bfloat16)
    return high, low


def dot(left, right, dims):
    return lax.dot_general(left, right, (dims, ((), ())), preferred_element_type=jnp.float32)


def dot3(left, right, dims):
    return (
        dot(left[0], right[0], dims)
        + dot(left[0], right[1], dims)
        + dot(left[1], right[0], dims)
    )


NT = ((1,), (1,))
NN = ((1,), (0,))


def kernel(
    dp_count, inner_count,
    img, txt, img_cluster_in, txt_cluster_in, txt_pair_in, scale_ref, bias_ref,
    grad_out, back_out,
    home, ids, visit, high, low, grad, visit_grad, meta, visit_meta, column,
    relay_out, relay_back,
    load_sem, store_sem, fwd_send, fwd_recv, meta_send, meta_recv,
    back_send, back_recv, relay_send, relay_recv, go_sem,
):
    rows, width = img.shape
    step = rows // CHUNKS
    a, k = lax.axis_index("dp"), lax.axis_index("inner")
    x = a % RUN
    run = a - x
    core = k % 2
    dp_next, dp_prev = (a + 1) % dp_count, (a + dp_count - 1) % dp_count
    in_next, in_prev = (k + 1) % inner_count, (k + inner_count - 1) % inner_count
    run_next, run_prev = (run + RUN) % dp_count, (run + dp_count - 1) % dp_count
    early, late = core, 1 - core
    scale, bias = scale_ref[0], bias_ref[0]

    loads = [
        pltpu.make_async_copy(img, home.at[0], load_sem.at[0]),
        pltpu.make_async_copy(txt, home.at[1], load_sem.at[1]),
        pltpu.make_async_copy(img_cluster_in, ids.at[0], load_sem.at[2]),
        pltpu.make_async_copy(txt_cluster_in, ids.at[1], load_sem.at[3]),
        pltpu.make_async_copy(txt_pair_in, ids.at[2], load_sem.at[4]),
    ]
    for load in loads:
        load.start()

    barrier = pltpu.get_barrier_semaphore()

    def greet(dp, inner):
        pl.semaphore_signal(barrier, inc=1, device_id=(dp, inner), device_id_type=MESH)

    for other in range(1, RUN):
        greet(run + (x + other) % RUN, k)
    greet(a, in_next)
    greet(a, in_prev)
    greet(run_next, k)
    greet(run_prev, k)

    @pl.when(x == 0)
    def _():
        for other in range(2, RUN + 1):
            greet((run + dp_count - other) % dp_count, k)

    @pl.when(x == RUN - 1)
    def _():
        for other in range(1, RUN):
            greet((run + RUN + other) % dp_count, k)

    row = lax.broadcasted_iota(jnp.int32, (8, rows), 0)
    number = (a * inner_count + k) * rows + lax.broadcasted_iota(jnp.int32, (8, rows), 1)
    for load in loads[2:]:
        load.wait()
    wide = lambda slot: jnp.broadcast_to(ids[slot], (8, rows))
    meta[0] = jnp.where(row == 0, number, wide(0)).astype(jnp.float32)
    meta[1] = jnp.where(row == 0, wide(2), wide(1)).astype(jnp.float32)

    end = (x == 0) | (x == RUN - 1)
    pl.semaphore_wait(barrier, jnp.where(end, 2 * RUN + 2, RUN + 3))

    def piece(chunk):
        return pl.ds(pl.multiple_of(chunk * step, step), step)

    def remote(src, dst, send, recv, dp, inner):
        return pltpu.make_async_remote_copy(
            src_ref=src, dst_ref=dst, send_sem=send, recv_sem=recv,
            device_id=(dp, inner), device_id_type=MESH,
        )

    meta_copies = [
        remote(meta.at[0], visit_meta.at[0], meta_send.at[0], meta_recv.at[0], dp_next, k),
        remote(meta.at[1], visit_meta.at[1], meta_send.at[1], meta_recv.at[1], a, in_next),
    ]

    def image_direct(chunk):
        return remote(
            img.at[piece(chunk)], visit.at[0, piece(chunk)],
            fwd_send.at[0, chunk], fwd_recv.at[0, chunk], dp_next, k,
        )

    def image_start(chunk):
        if chunk == CHUNKS - 1:
            image_direct(chunk).start()
            return

        @pl.when(x < RUN - 1)
        def _():
            image_direct(chunk).start()

        @pl.when(x == RUN - 1)
        def _():
            remote(
                img.at[piece(chunk)], relay_out,
                fwd_send.at[0, chunk], relay_recv.at[0], run + chunk, k,
            ).start()

    def text_copy(chunk):
        return remote(
            txt.at[piece(chunk)], visit.at[1, piece(chunk)],
            fwd_send.at[1, chunk], fwd_recv.at[1, chunk], a, in_next,
        )

    def relay_out_copy():
        return remote(
            relay_out, visit.at[0, piece(x)],
            relay_send.at[0], fwd_recv.at[0, x], run_next, k,
        )

    def relay_out_step():
        @pl.when(x < RUN - 1)
        def _():
            remote(relay_out, relay_out, relay_send.at[0], relay_recv.at[0], run_next, k).wait_recv()
            relay_out_copy().start()

    def image_back_direct(chunk):
        return remote(
            visit_grad.at[0, piece(chunk)], back_out.at[0, piece(chunk)],
            back_send.at[0, chunk], back_recv.at[0, chunk], dp_prev, k,
        )

    def image_back_start(chunk):
        aside = (x == 0) & (chunk < CHUNKS - 1)

        @pl.when(jnp.logical_not(aside))
        def _():
            image_back_direct(chunk).start()

        @pl.when(aside)
        def _():
            remote(
                visit_grad.at[0, piece(chunk)], relay_back,
                back_send.at[0, chunk], relay_recv.at[1], run + chunk + 1, k,
            ).start()

    def relay_back_copy():
        chunk = (x + CHUNKS - 1) % CHUNKS
        return remote(
            relay_back, back_out.at[0, piece(chunk)],
            relay_send.at[1], back_recv.at[0, chunk], run_prev, k,
        )

    def relay_back_step():
        @pl.when(x > 0)
        def _():
            remote(relay_back, relay_back, relay_send.at[1], relay_recv.at[1], run_prev, k).wait_recv()
            relay_back_copy().start()

    def text_back(chunk):
        return remote(
            visit_grad.at[1, piece(chunk)], back_out.at[1, piece(chunk)],
            back_send.at[1, chunk], back_recv.at[1, chunk], a, in_prev,
        )

    def fwd_wait(which, chunk):
        pltpu.make_async_copy(
            visit.at[which, piece(chunk)], visit.at[which, piece(chunk)], fwd_recv.at[which, chunk]
        ).wait()

    def weights(logits, left, right):
        logits = scale * logits + bias
        positive = left[:, 0:1] == right[0:1, :]
        other = left[:, 1:2] != right[1:2, :]
        sig = jax.nn.sigmoid(jnp.where(positive, -logits, logits))
        return scale * jnp.where(positive, -sig, jnp.where(other, sig, 0.0))

    for copy in meta_copies:
        copy.start()

    @pl.when(core == 0)
    def _():
        for chunk in range(CHUNKS):
            image_start(chunk)

    for chunk in range(CHUNKS):
        text_copy(chunk).start()

    @pl.when((core == 1) & (x == RUN - 1))
    def _():
        for chunk in range(CHUNKS):
            image_start(chunk)

    near, far = pl.ds(0, rows), pl.ds(rows, rows)
    for which in range(2):
        loads[which].wait()
        high[which, near], low[which, near] = split(home[which])
    early_near = (high[early, near], low[early, near])
    late_near = (high[late, near], low[late, near])
    column[0] = jnp.transpose(meta[late])
    pair = weights(dot3(late_near, early_near, NT), column[0], meta[early])
    grad[late] = dot3(split(pair), early_near, NN)
    grad[early] = dot3(split(pair.T), late_near, NN)

    @pl.when(core == 0)
    def _():
        relay_out_step()
        for chunk in range(CHUNKS):
            image_direct(chunk).wait_send()

        @pl.when(x < RUN - 1)
        def _():
            pl.semaphore_signal(go_sem, inc=1, device_id=(a, in_next), device_id_type=MESH)

    pltpu.make_async_copy(visit_meta.at[early], visit_meta.at[early], meta_recv.at[early]).wait()
    for chunk in range(CHUNKS):
        fwd_wait(early, chunk)
    high[early, far], low[early, far] = split(visit[early])
    early_far = (high[early, far], low[early, far])
    late_near = (high[late, near], low[late, near])
    pair = weights(dot3(late_near, early_far, NT), column[0], visit_meta[early])
    grad[late] += dot3(split(pair), early_far, NN)
    visit_grad[early] = dot3(split(pair.T), late_near, NN)

    @pl.when(core == 1)
    def _():
        @pl.when(x < RUN - 1)
        def _():
            pl.semaphore_wait(go_sem, 1)
            for chunk in range(CHUNKS):
                image_direct(chunk).start()

        relay_out_step()

    pltpu.make_async_copy(visit_meta.at[late], visit_meta.at[late], meta_recv.at[late]).wait()
    column[1] = jnp.transpose(visit_meta[late])

    def late_chunk(chunk, carry):
        fwd_wait(late, chunk)
        here = piece(chunk)
        part = split(visit[late, here])
        both = (high[early], low[early])
        right = jnp.concatenate([meta[early], visit_meta[early]], axis=1)
        pair = weights(dot3(part, both, NT), column[1, here], right)
        visit_grad[late, here] = dot3(split(pair), both, NN)

        @pl.when(core == 0)
        def _():
            text_back(chunk).start()

        @pl.when(core == 1)
        def _():
            image_back_start(chunk)

        turned = split(pair.T)
        visit_grad[early] += dot3((turned[0][rows:], turned[1][rows:]), part, NN)
        grad[early] += dot3((turned[0][:rows], turned[1][:rows]), part, NN)
        return carry

    lax.fori_loop(0, CHUNKS, late_chunk, 0)

    @pl.when(core == 0)
    def _():
        for chunk in range(CHUNKS):
            if chunk == CHUNKS // 2:

                @pl.when(x < RUN - 1)
                def _():
                    relay_back_step()

            image_back_start(chunk)

    @pl.when(core == 1)
    def _():
        for chunk in range(CHUNKS):
            text_back(chunk).start()
        relay_back_step()

    store = pltpu.make_async_copy(grad, grad_out, store_sem)
    store.start()

    @pl.when((core == 0) & (x == RUN - 1))
    def _():
        relay_back_step()

    for which in range(2):
        for chunk in range(CHUNKS):
            pltpu.make_async_copy(
                back_out.at[which, piece(chunk)], back_out.at[which, piece(chunk)],
                back_recv.at[which, chunk],
            ).wait()

    @pl.when(core == 1)
    def _():
        for chunk in range(CHUNKS):
            image_direct(chunk).wait_send()

    for chunk in range(CHUNKS):
        text_copy(chunk).wait_send()
        text_back(chunk).wait_send()
        image_back_direct(chunk).wait_send()
    for copy in meta_copies:
        copy.wait_send()

    @pl.when(x < RUN - 1)
    def _():
        relay_out_copy().wait_send()

    @pl.when(x > 0)
    def _():
        relay_back_copy().wait_send()

    store.wait()


def body(images, texts, image_cluster, text_cluster, text_pair, logit_scale, logit_bias):
    rows, width = images.shape
    step = rows // CHUNKS
    dp_count, inner_count = lax.axis_size("dp"), lax.axis_size("inner")
    dma = pltpu.SemaphoreType.DMA
    f32, bf16 = jnp.float32, jnp.bfloat16
    hbm, free, smem = (
        pl.BlockSpec(memory_space=space) for space in (pltpu.HBM, pl.ANY, pltpu.SMEM)
    )
    grads = jax.ShapeDtypeStruct((2, rows, width), f32)
    held = lambda value: pltpu.with_memory_space_constraint(value, pltpu.HBM)
    own, back = pl.pallas_call(
        functools.partial(kernel, dp_count, inner_count),
        out_shape=(grads, grads),
        in_specs=[hbm] * 5 + [smem] * 2,
        out_specs=(free, free),
        scratch_shapes=[
            pltpu.VMEM((2, rows, width), f32),
            pltpu.VMEM((3, 1, rows), jnp.int32),
            pltpu.VMEM((2, rows, width), f32),
            pltpu.VMEM((2, 2 * rows, width), bf16),
            pltpu.VMEM((2, 2 * rows, width), bf16),
            pltpu.VMEM((2, rows, width), f32),
            pltpu.VMEM((2, rows, width), f32),
            pltpu.VMEM((2, 8, rows), f32),
            pltpu.VMEM((2, 8, rows), f32),
            pltpu.VMEM((2, rows, 8), f32),
            pltpu.VMEM((step, width), f32),
            pltpu.VMEM((step, width), f32),
            dma((5,)),
            dma,
            dma((2, CHUNKS)),
            dma((2, CHUNKS)),
            dma((2,)),
            dma((2,)),
            dma((2, CHUNKS)),
            dma((2, CHUNKS)),
            dma((2,)),
            dma((2,)),
            pltpu.SemaphoreType.REGULAR,
        ],
        compiler_params=pltpu.CompilerParams(
            collective_id=0, has_side_effects=True, vmem_limit_bytes=32 * 1024 * 1024
        ),
        cost_estimate=pl.CostEstimate(
            flops=24 * rows * rows * width, bytes_accessed=24 * rows * width, transcendentals=0
        ),
    )(
        held(images), held(texts),
        held(image_cluster.reshape(1, rows)),
        held(text_cluster.reshape(1, rows)),
        held(text_pair.reshape(1, rows)),
        logit_scale.reshape(1), logit_bias.reshape(1),
    )
    return (own[0] + back[0], own[1] + back[1])


def solution(mesh):
    return jax.shard_map(
        body,
        mesh=mesh,
        in_specs=(
            P(("dp", "inner"), None),
            P(("dp", "inner"), None),
            P(("dp", "inner")),
            P(("dp", "inner")),
            P(("dp", "inner")),
            P(),
            P(),
        ),
        out_specs=(P(("dp", "inner"), None), P(("dp", "inner"), None)),
        check_vma=False,
    )
```

```python
import functools

import jax
import jax.numpy as jnp
from jax import lax
from jax.experimental import pallas as pl
from jax.experimental.pallas import tpu as pltpu
from jax.sharding import PartitionSpec as P

MESH = pl.DeviceIdType.MESH
CHUNKS = 4
RUN = 4


def split(value):
    high = value.astype(jnp.bfloat16)
    low = (value - high.astype(jnp.float32)).astype(jnp.bfloat16)
    return high, low


def dot(left, right, dims):
    return lax.dot_general(left, right, (dims, ((), ())), preferred_element_type=jnp.float32)


def dot3(left, right, dims):
    return (
        dot(left[0], right[0], dims)
        + dot(left[0], right[1], dims)
        + dot(left[1], right[0], dims)
    )


NT = ((1,), (1,))
NN = ((1,), (0,))


def kernel(
    dp_count, inner_count,
    img, txt, img_cluster_in, txt_cluster_in, txt_pair_in, scale_ref, bias_ref,
    grad_out, back_out,
    home, ids, visit, high, low, grad, visit_grad, meta, visit_meta, column,
    relay_out, relay_back,
    load_sem, store_sem, fwd_send, fwd_recv, meta_send, meta_recv,
    back_send, back_recv, relay_send, relay_recv, go_sem,
):
    rows, width = img.shape
    step = rows // CHUNKS
    a, k = lax.axis_index("dp"), lax.axis_index("inner")
    x = a % RUN
    run = a - x
    core = k % 2
    dp_next, dp_prev = (a + 1) % dp_count, (a + dp_count - 1) % dp_count
    in_next, in_prev = (k + 1) % inner_count, (k + inner_count - 1) % inner_count
    run_next, run_prev = (run + RUN) % dp_count, (run + dp_count - 1) % dp_count
    early, late = core, 1 - core
    scale, bias = scale_ref[0], bias_ref[0]

    loads = [
        pltpu.make_async_copy(img, home.at[0], load_sem.at[0]),
        pltpu.make_async_copy(txt, home.at[1], load_sem.at[1]),
        pltpu.make_async_copy(img_cluster_in, ids.at[0], load_sem.at[2]),
        pltpu.make_async_copy(txt_cluster_in, ids.at[1], load_sem.at[3]),
        pltpu.make_async_copy(txt_pair_in, ids.at[2], load_sem.at[4]),
    ]
    for load in loads:
        load.start()

    barrier = pltpu.get_barrier_semaphore()

    def greet(dp, inner):
        pl.semaphore_signal(barrier, inc=1, device_id=(dp, inner), device_id_type=MESH)

    for other in range(1, RUN):
        greet(run + (x + other) % RUN, k)
    greet(a, in_next)
    greet(a, in_prev)
    greet(run_next, k)
    greet(run_prev, k)

    @pl.when(x == 0)
    def _():
        for other in range(2, RUN + 1):
            greet((run + dp_count - other) % dp_count, k)

    @pl.when(x == RUN - 1)
    def _():
        for other in range(1, RUN):
            greet((run + RUN + other) % dp_count, k)

    row = lax.broadcasted_iota(jnp.int32, (8, rows), 0)
    number = (a * inner_count + k) * rows + lax.broadcasted_iota(jnp.int32, (8, rows), 1)
    for load in loads[2:]:
        load.wait()
    wide = lambda slot: jnp.broadcast_to(ids[slot], (8, rows))
    meta[0] = jnp.where(row == 0, number, wide(0)).astype(jnp.float32)
    meta[1] = jnp.where(row == 0, wide(2), wide(1)).astype(jnp.float32)

    end = (x == 0) | (x == RUN - 1)
    pl.semaphore_wait(barrier, jnp.where(end, 2 * RUN + 2, RUN + 3))

    def piece(chunk):
        return pl.ds(pl.multiple_of(chunk * step, step), step)

    def remote(src, dst, send, recv, dp, inner):
        return pltpu.make_async_remote_copy(
            src_ref=src, dst_ref=dst, send_sem=send, recv_sem=recv,
            device_id=(dp, inner), device_id_type=MESH,
        )

    meta_copies = [
        remote(meta.at[0], visit_meta.at[0], meta_send.at[0], meta_recv.at[0], dp_next, k),
        remote(meta.at[1], visit_meta.at[1], meta_send.at[1], meta_recv.at[1], a, in_next),
    ]

    def image_direct(chunk):
        return remote(
            img.at[piece(chunk)], visit.at[0, piece(chunk)],
            fwd_send.at[0, chunk], fwd_recv.at[0, chunk], dp_next, k,
        )

    def image_start(chunk):
        if chunk == CHUNKS - 1:
            image_direct(chunk).start()
            return

        @pl.when(x < RUN - 1)
        def _():
            image_direct(chunk).start()

        @pl.when(x == RUN - 1)
        def _():
            remote(
                img.at[piece(chunk)], relay_out,
                fwd_send.at[0, chunk], relay_recv.at[0], run + chunk, k,
            ).start()

    def text_copy(chunk):
        return remote(
            txt.at[piece(chunk)], visit.at[1, piece(chunk)],
            fwd_send.at[1, chunk], fwd_recv.at[1, chunk], a, in_next,
        )

    def relay_out_copy():
        return remote(
            relay_out, visit.at[0, piece(x)],
            relay_send.at[0], fwd_recv.at[0, x], run_next, k,
        )

    def relay_out_step():
        @pl.when(x < RUN - 1)
        def _():
            remote(relay_out, relay_out, relay_send.at[0], relay_recv.at[0], run_next, k).wait_recv()
            relay_out_copy().start()

    def image_back_direct(chunk):
        return remote(
            visit_grad.at[0, piece(chunk)], back_out.at[0, piece(chunk)],
            back_send.at[0, chunk], back_recv.at[0, chunk], dp_prev, k,
        )

    def image_back_start(chunk):
        aside = (x == 0) & (chunk < CHUNKS - 1)

        @pl.when(jnp.logical_not(aside))
        def _():
            image_back_direct(chunk).start()

        @pl.when(aside)
        def _():
            remote(
                visit_grad.at[0, piece(chunk)], relay_back,
                back_send.at[0, chunk], relay_recv.at[1], run + chunk + 1, k,
            ).start()

    def relay_back_copy():
        chunk = (x + CHUNKS - 1) % CHUNKS
        return remote(
            relay_back, back_out.at[0, piece(chunk)],
            relay_send.at[1], back_recv.at[0, chunk], run_prev, k,
        )

    def relay_back_step():
        @pl.when(x > 0)
        def _():
            remote(relay_back, relay_back, relay_send.at[1], relay_recv.at[1], run_prev, k).wait_recv()
            relay_back_copy().start()

    def text_back(chunk):
        return remote(
            visit_grad.at[1, piece(chunk)], back_out.at[1, piece(chunk)],
            back_send.at[1, chunk], back_recv.at[1, chunk], a, in_prev,
        )

    def fwd_wait(which, chunk):
        pltpu.make_async_copy(
            visit.at[which, piece(chunk)], visit.at[which, piece(chunk)], fwd_recv.at[which, chunk]
        ).wait()

    def weights(logits, left, right):
        logits = scale * logits + bias
        positive = left[:, 0:1] == right[0:1, :]
        other = left[:, 1:2] != right[1:2, :]
        sig = jax.nn.sigmoid(jnp.where(positive, -logits, logits))
        return scale * jnp.where(positive, -sig, jnp.where(other, sig, 0.0))

    for copy in meta_copies:
        copy.start()

    @pl.when((core == 0) | (x == RUN - 1))
    def _():
        for chunk in range(CHUNKS):
            image_start(chunk)

    for chunk in range(CHUNKS):
        text_copy(chunk).start()

    near, far = pl.ds(0, rows), pl.ds(rows, rows)
    for which in range(2):
        loads[which].wait()
        high[which, near], low[which, near] = split(home[which])
    early_near = (high[early, near], low[early, near])
    late_near = (high[late, near], low[late, near])
    column[0] = jnp.transpose(meta[late])
    pair = weights(dot3(late_near, early_near, NT), column[0], meta[early])
    grad[late] = dot3(split(pair), early_near, NN)
    grad[early] = dot3(split(pair.T), late_near, NN)

    @pl.when(core == 0)
    def _():
        relay_out_step()
        for chunk in range(CHUNKS):
            image_direct(chunk).wait_send()

        @pl.when(x < RUN - 1)
        def _():
            pl.semaphore_signal(go_sem, inc=1, device_id=(a, in_next), device_id_type=MESH)

    pltpu.make_async_copy(visit_meta.at[early], visit_meta.at[early], meta_recv.at[early]).wait()
    for chunk in range(CHUNKS):
        fwd_wait(early, chunk)
    high[early, far], low[early, far] = split(visit[early])
    early_far = (high[early, far], low[early, far])
    late_near = (high[late, near], low[late, near])
    pair = weights(dot3(late_near, early_far, NT), column[0], visit_meta[early])
    grad[late] += dot3(split(pair), early_far, NN)
    visit_grad[early] = dot3(split(pair.T), late_near, NN)

    @pl.when(core == 1)
    def _():
        relay_out_step()

        @pl.when(x < RUN - 1)
        def _():
            pl.semaphore_wait(go_sem, 1)
            for chunk in range(CHUNKS):
                image_direct(chunk).start()

    pltpu.make_async_copy(visit_meta.at[late], visit_meta.at[late], meta_recv.at[late]).wait()
    column[1] = jnp.transpose(visit_meta[late])

    def late_chunk(chunk, carry):
        fwd_wait(late, chunk)
        here = piece(chunk)
        part = split(visit[late, here])
        both = (high[early], low[early])
        right = jnp.concatenate([meta[early], visit_meta[early]], axis=1)
        pair = weights(dot3(part, both, NT), column[1, here], right)
        visit_grad[late, here] = dot3(split(pair), both, NN)

        @pl.when(core == 0)
        def _():
            text_back(chunk).start()

        @pl.when(core == 1)
        def _():
            image_back_start(chunk)

        turned = split(pair.T)
        visit_grad[early] += dot3((turned[0][rows:], turned[1][rows:]), part, NN)
        grad[early] += dot3((turned[0][:rows], turned[1][:rows]), part, NN)
        return carry

    lax.fori_loop(0, CHUNKS, late_chunk, 0)

    @pl.when(core == 1)
    def _():
        relay_back_step()

    @pl.when(core == 0)
    def _():
        for chunk in range(CHUNKS):
            image_back_start(chunk)

    @pl.when(core == 1)
    def _():
        for chunk in range(CHUNKS):
            text_back(chunk).start()

    store = pltpu.make_async_copy(grad, grad_out, store_sem)
    store.start()

    @pl.when(core == 0)
    def _():
        relay_back_step()

    for which in range(2):
        for chunk in range(CHUNKS):
            pltpu.make_async_copy(
                back_out.at[which, piece(chunk)], back_out.at[which, piece(chunk)],
                back_recv.at[which, chunk],
            ).wait()

    @pl.when(core == 1)
    def _():
        for chunk in range(CHUNKS):
            image_direct(chunk).wait_send()

    for chunk in range(CHUNKS):
        text_copy(chunk).wait_send()
        text_back(chunk).wait_send()
        image_back_direct(chunk).wait_send()
    for copy in meta_copies:
        copy.wait_send()

    @pl.when(x < RUN - 1)
    def _():
        relay_out_copy().wait_send()

    @pl.when(x > 0)
    def _():
        relay_back_copy().wait_send()

    store.wait()


def body(images, texts, image_cluster, text_cluster, text_pair, logit_scale, logit_bias):
    rows, width = images.shape
    step = rows // CHUNKS
    dp_count, inner_count = lax.axis_size("dp"), lax.axis_size("inner")
    dma = pltpu.SemaphoreType.DMA
    f32, bf16 = jnp.float32, jnp.bfloat16
    hbm, free, smem = (
        pl.BlockSpec(memory_space=space) for space in (pltpu.HBM, pl.ANY, pltpu.SMEM)
    )
    grads = jax.ShapeDtypeStruct((2, rows, width), f32)
    held = lambda value: pltpu.with_memory_space_constraint(value, pltpu.HBM)
    own, back = pl.pallas_call(
        functools.partial(kernel, dp_count, inner_count),
        out_shape=(grads, grads),
        in_specs=[hbm] * 5 + [smem] * 2,
        out_specs=(free, free),
        scratch_shapes=[
            pltpu.VMEM((2, rows, width), f32),
            pltpu.VMEM((3, 1, rows), jnp.int32),
            pltpu.VMEM((2, rows, width), f32),
            pltpu.VMEM((2, 2 * rows, width), bf16),
            pltpu.VMEM((2, 2 * rows, width), bf16),
            pltpu.VMEM((2, rows, width), f32),
            pltpu.VMEM((2, rows, width), f32),
            pltpu.VMEM((2, 8, rows), f32),
            pltpu.VMEM((2, 8, rows), f32),
            pltpu.VMEM((2, rows, 8), f32),
            pltpu.VMEM((step, width), f32),
            pltpu.VMEM((step, width), f32),
            dma((5,)),
            dma,
            dma((2, CHUNKS)),
            dma((2, CHUNKS)),
            dma((2,)),
            dma((2,)),
            dma((2, CHUNKS)),
            dma((2, CHUNKS)),
            dma((2,)),
            dma((2,)),
            pltpu.SemaphoreType.REGULAR,
        ],
        compiler_params=pltpu.CompilerParams(
            collective_id=0, has_side_effects=True, vmem_limit_bytes=32 * 1024 * 1024
        ),
        cost_estimate=pl.CostEstimate(
            flops=24 * rows * rows * width, bytes_accessed=24 * rows * width, transcendentals=0
        ),
    )(
        held(images), held(texts),
        held(image_cluster.reshape(1, rows)),
        held(text_cluster.reshape(1, rows)),
        held(text_pair.reshape(1, rows)),
        logit_scale.reshape(1), logit_bias.reshape(1),
    )
    return (own[0] + back[0], own[1] + back[1])


def solution(mesh):
    return jax.shard_map(
        body,
        mesh=mesh,
        in_specs=(
            P(("dp", "inner"), None),
            P(("dp", "inner"), None),
            P(("dp", "inner")),
            P(("dp", "inner")),
            P(("dp", "inner")),
            P(),
            P(),
        ),
        out_specs=(P(("dp", "inner"), None), P(("dp", "inner"), None)),
        check_vma=False,
    )
```
